128 devices in a mesh: dp: 8 (over y, core), mp: 16 (over x, z).
Axes of the slice: x: 4, y: 4, z: 4, core: 2. Of those that a mesh axis runs over, the one named last changes fastest.
Arguments:
- activations: bfloat16 [2, 2048, 4096], P(None, 'dp'), may hold values from -6 to 6
- cotangents: bfloat16 [2, 2048, 24576], P(None, 'dp', 'mp'), may hold values from -0.3125 to 0.3125
- left_root: bfloat16 [8, 16, 8, 512, 512], P('dp', 'mp')
- right_root: bfloat16 [8, 16, 8, 512, 512], P('dp', 'mp')
- block_owner: int32 [8, 16, 6], P('dp', 'mp'), may hold values from 0 to 15, as said below
- owned_sources: int32 [8, 16, 8], P('dp', 'mp'), may hold values from -1 to 15, as said below
- owner_counts: int32 [8, 16], P('dp', 'mp'), may hold values from 5 to 8, as said below
Outputs:
- precond: bfloat16 [2, 4096, 24576], P(None, 'dp', 'mp')
- left_stats: bfloat16 [8, 16, 8, 512, 512], P('dp', 'mp')
- right_stats: bfloat16 [8, 16, 8, 512, 512], P('dp', 'mp')
The draws below stay inside these ranges and needn't reach their ends.
Inputs may be any that keep to these rules, and one draw needn't show every extreme that they name: In each group g no holder names one owner for two of its blocks; block_owner, owned_sources and owner_counts describe one assignment of the group's 6 x mp blocks. owned_sources[g, o, s] is the holder of owner o's s-th block, holders ascending, for s < owner_counts[g, o], and -1 after. `owner_counts`: in each group one owner holds exactly 8 blocks.
All inputs are finite; a program needn't handle non-finite values.
Results may differ from the reference program's by a relative error of at most 0.02.
Values may be sent and summed in bfloat16 or wider, within the bound.
No kernel may reach another device: no remote copies, remote signals or barrier semaphores. Data moves between devices by JAX's collectives and lax.ppermute only.
A program may use at most 192 MiB of HBM per device.

```python
import math
import jax
import jax.numpy as jnp
from jax import lax

TOK_DEV = 256
LAYERS = 2
BLK = 512
ROW_BLOCKS = 1
COL_DEV = 1536
D_WIN = 4096
TOKENS = 2048
COLS = 24576
COL_BLOCKS = 3
BPD = 6
CAP = 8
N_DP = 8
N_MP = 16


def routing_tables(key):
    group_keys = jax.random.split(key, N_DP)

    def one_group(group_key):
        shuffle = jax.random.permutation(group_key, N_MP).astype(jnp.int32)
        holder_index = jnp.arange(N_MP, dtype=jnp.int32)[:, None]
        turn_index = jnp.arange(BPD, dtype=jnp.int32)[None, :]
        position = (holder_index + turn_index) % N_MP
        redirect = (turn_index == 0) & (holder_index >= 1) & (holder_index <= CAP - BPD)
        position = jnp.where(redirect, 0, position)
        owner_table = shuffle[position]
        owner_range = jnp.arange(N_MP, dtype=jnp.int32)
        member = jnp.any(owner_table[:, :, None] == owner_range[None, None, :], axis=1).astype(jnp.int32)
        counts_now = jnp.sum(member, axis=0)
        ranking = jnp.cumsum(member, axis=0) - 1
        slot_range = jnp.arange(CAP, dtype=jnp.int32)
        matched = (member[:, :, None] == 1) & (ranking[:, :, None] == slot_range[None, None, :])
        holder_list = jnp.sum(jnp.where(matched, holder_index[:, :, None], 0), axis=0)
        holder_list = jnp.where(slot_range[None, :] < counts_now[:, None], holder_list, -1)
        return (owner_table.astype(jnp.int32), holder_list.astype(jnp.int32), counts_now.astype(jnp.int32))
    return jax.vmap(one_group)(group_keys)


def root_matrix(key, random_part):
    diagonal_key = jax.random.fold_in(key, 1)
    diagonal = jnp.exp(jax.random.uniform(diagonal_key, (N_DP, N_MP, CAP, BLK), jnp.float32, math.log(0.5), math.log(2.0)))
    row_index = lax.broadcasted_iota(jnp.int32, (BLK, BLK), 0)
    col_index = lax.broadcasted_iota(jnp.int32, (BLK, BLK), 1)
    identity_mask = (row_index == col_index).astype(jnp.float32)
    return (identity_mask * diagonal[..., :, None] + random_part * (0.6 / math.sqrt(BLK))).astype(jnp.bfloat16)


def draw_left_root(key, part):
    key = jax.random.fold_in(key, 11)
    noise_key = jax.random.fold_in(key, 2)
    full_shape = (N_DP, N_MP, CAP, BLK, BLK)
    random_part = jax.random.normal(noise_key, full_shape, jnp.float32)
    return root_matrix(key, random_part)


def draw_right_root(key, part):
    key = jax.random.fold_in(key, 12)
    noise_key = jax.random.fold_in(key, 2)
    full_shape = (N_DP, N_MP, CAP, BLK, BLK)
    random_part = jax.random.normal(noise_key, full_shape, jnp.float32)
    return root_matrix(key, random_part)


def draw_block_owner(key, part):
    return routing_tables(key)[0]


def draw_owned_sources(key, part):
    return routing_tables(key)[1]


def draw_owner_counts(key, part):
    return routing_tables(key)[2]


def block_levels(key, dims, cuts, low, top_value):
    def one(dim, blocks):
        draws = jax.random.uniform(jax.random.fold_in(jax.random.fold_in(key, 6), dim), (blocks,), jnp.float32, low / len(cuts), top_value / len(cuts))
        return jnp.repeat(jnp.exp(draws), dims[dim] // blocks).reshape((-1,) + (1,) * (len(dims) - dim - 1))

    loudness = one(*cuts[0])
    for cut in cuts[1:]:
        loudness = loudness * one(*cut)
    return loudness


def gaussian(own_key, shape, scale, limit, cuts=(), kind=jnp.bfloat16):
    gain = block_levels(own_key, shape, cuts, -0.22, 0.18) if cuts else 1.0
    entries = jax.random.normal(own_key, shape, jnp.float32) * scale * gain
    return jnp.minimum(jnp.maximum(entries, -limit), limit).astype(kind)


def setup_inputs(seed: int = 0) -> dict:
    key_of = jax.random.split(jax.random.key(seed), 8)
    return {
        "activations": gaussian(key_of[0], (LAYERS, TOKENS, D_WIN), 1.0, 6.0, ((1, 8),)),
        "cotangents": gaussian(key_of[1], (LAYERS, TOKENS, COLS), ((TOK_DEV * N_DP) ** -0.5), 0.3125, ((1, 8), (2, 16))),
        "left_root": draw_left_root(jax.random.fold_in(key_of[7], 71), 0),
        "right_root": draw_right_root(jax.random.fold_in(key_of[7], 71), 0),
        "block_owner": draw_block_owner(jax.random.fold_in(key_of[7], 71), 0),
        "owned_sources": draw_owned_sources(jax.random.fold_in(key_of[7], 71), 0),
        "owner_counts": draw_owner_counts(jax.random.fold_in(key_of[7], 71), 0),
    }


def reference(activations, cotangents, left_root, right_root, block_owner, owned_sources, owner_counts):
    highest = lax.Precision.HIGHEST
    act_groups = activations.reshape(LAYERS, N_DP, TOK_DEV, D_WIN).transpose(1, 0, 2, 3)
    cot_groups = cotangents.reshape(LAYERS, N_DP, TOK_DEV, COL_DEV * N_MP).transpose(1, 0, 2, 3)

    def add_group(total, inputs):
        act_part, cot_part = inputs
        partial_value = jnp.einsum("ltd,ltc->ldc", act_part.astype(jnp.float32), cot_part.astype(jnp.float32), precision=highest)
        rounded = lax.optimization_barrier(partial_value.astype(jnp.bfloat16))
        return total + rounded.astype(jnp.float32), None

    start_total = jnp.zeros((LAYERS, D_WIN, COL_DEV * N_MP), jnp.float32)
    gradient, _ = lax.scan(add_group, start_total, (act_groups, cot_groups))
    held_grad = gradient.astype(jnp.bfloat16)
    blocks = held_grad.reshape(LAYERS, N_DP, ROW_BLOCKS, BLK, N_MP, COL_BLOCKS, BLK).transpose(1, 4, 0, 2, 5, 3, 6).reshape(N_DP, N_MP, BPD, BLK, BLK)
    group_index = jnp.arange(N_DP, dtype=jnp.int32)[:, None, None]
    holder_index = jnp.arange(N_MP, dtype=jnp.int32)[None, :, None]
    slot_range = jnp.arange(CAP, dtype=jnp.int32)
    owner_lists = owned_sources[group_index, block_owner]
    slot_of = jnp.sum(jnp.where(owner_lists == holder_index[..., None], slot_range, 0), axis=-1).astype(jnp.int32)
    left_held = left_root[group_index, block_owner, slot_of]
    right_held = right_root[group_index, block_owner, slot_of]

    def per_group(inputs):
        grad_blocks, left_blocks, right_blocks = inputs
        values = grad_blocks.astype(jnp.float32)
        left_gram = jnp.einsum("hsab,hscb->hsac", values, values, precision=highest) / BLK
        right_gram = jnp.einsum("hsba,hsbc->hsac", values, values, precision=highest) / BLK
        inner_prod = jnp.einsum("hsab,hsbc->hsac", left_blocks.astype(jnp.float32), values, precision=highest).astype(jnp.bfloat16)
        result = jnp.einsum("hsab,hsbc->hsac", inner_prod.astype(jnp.float32), right_blocks.astype(jnp.float32), precision=highest).astype(jnp.bfloat16)
        return left_gram, right_gram, result

    left_gram, right_gram, result = lax.map(per_group, (blocks, left_held, right_held))
    precond = result.reshape(N_DP, N_MP, LAYERS, ROW_BLOCKS, COL_BLOCKS, BLK, BLK).transpose(2, 0, 3, 5, 1, 4, 6).reshape(LAYERS, D_WIN, COL_DEV * N_MP)
    holders = jnp.maximum(owned_sources, 0)
    sender_owner = block_owner[group_index, holders]
    owner_index = jnp.arange(N_MP, dtype=jnp.int32)[None, :, None, None]
    turn_range = jnp.arange(BPD, dtype=jnp.int32)
    turn_of = jnp.sum(jnp.where(sender_owner == owner_index, turn_range, 0), axis=-1).astype(jnp.int32)
    live_slots = slot_range[None, None, :] < owner_counts[:, :, None]
    left_stats = jnp.where(live_slots[..., None, None], left_gram[group_index, holders, turn_of], 0.0).astype(jnp.bfloat16)
    right_stats = jnp.where(live_slots[..., None, None], right_gram[group_index, holders, turn_of], 0.0).astype(jnp.bfloat16)
    return precond, left_stats, right_stats
```

```python
import functools

import jax
import jax.numpy as jnp
from jax import lax
from jax.experimental import pallas as pl
from jax.experimental.pallas import tpu as pltpu
from jax.sharding import PartitionSpec as P

CHUNKS = 2
SIDE = 4
CORES = 2
TABLE_ROWS = 16
MIB = 1024 * 1024

NT = (((1,), (1,)), ((), ()))
NN = (((1,), (0,)), ((), ()))
TN = (((0,), (0,)), ((), ()))


def dot(a, b, dims):
    return lax.dot_general(a, b, dims, preferred_element_type=jnp.float32)


def along_y(value, hops):
    pairs = [
        (y * CORES + c, (y + hops) % SIDE * CORES + c) for y in range(SIDE) for c in range(CORES)
    ]
    return lax.ppermute(value, "dp", pairs)


def other_core(value):
    pairs = [(y * CORES + c, y * CORES + 1 - c) for y in range(SIDE) for c in range(CORES)]
    return lax.ppermute(value, "dp", pairs)


def along_x(value, hops):
    pairs = [(x * SIDE + z, (x + hops) % SIDE * SIDE + z) for x in range(SIDE) for z in range(SIDE)]
    return lax.ppermute(value, "mp", pairs)


def along_z(value, hops):
    pairs = [(x * SIDE + z, x * SIDE + (z + hops) % SIDE) for x in range(SIDE) for z in range(SIDE)]
    return lax.ppermute(value, "mp", pairs)


def ring(value, move):
    return (value, move(value, 1), move(value, -1), move(value, 2))


def exchange(value):
    return lax.all_to_all(value, "mp", split_axis=0, concat_axis=0, tiled=True)


def after(value, *needed):
    return lax.optimization_barrier((value,) + needed)[0]


def split_kernel(owner_ref, cot_ref, out_ref):
    layers, tokens, width = cot_ref.shape
    parts, piece = out_ref.shape[0], TABLE_ROWS
    size = parts * piece * CHUNKS
    cols = width // size
    for layer in range(layers):
        for col in range(cols):
            turned = cot_ref[layer, :, col * size : (col + 1) * size].T
            for q in range(CHUNKS):
                row = ((q * layers + layer) * cols + col) * piece
                half = turned[q * parts * piece : (q + 1) * parts * piece]
                out_ref[:, row : row + piece, :] = half.reshape(parts, piece, tokens)
    rows = lax.broadcasted_iota(jnp.int32, (TABLE_ROWS, tokens), 0)
    table = jnp.zeros((TABLE_ROWS, tokens), jnp.float32)
    for t in range(layers * cols):
        table = jnp.where(rows == t, owner_ref[t].astype(jnp.float32), table)
    base = CHUNKS * layers * cols * piece
    for part in range(parts):
        out_ref[part, base : base + TABLE_ROWS, :] = table.astype(out_ref.dtype)


def split_cotangents(owners, cotangents, owner_total):
    layers, tokens, width = cotangents.shape
    rows = width * layers // owner_total
    return pl.pallas_call(
        split_kernel,
        in_specs=[
            pl.BlockSpec(memory_space=pltpu.SMEM),
            pl.BlockSpec(memory_space=pltpu.VMEM),
        ],
        out_specs=pl.BlockSpec(memory_space=pltpu.VMEM),
        out_shape=jax.ShapeDtypeStruct((owner_total, rows + TABLE_ROWS, tokens), cotangents.dtype),
        compiler_params=pltpu.CompilerParams(vmem_limit_bytes=12 * MIB),
        cost_estimate=pl.CostEstimate(
            flops=0, bytes_accessed=4 * cotangents.size, transcendentals=0
        ),
        name="split_cotangents",
    )(owners, cotangents)


def lay_kernel(place_ref, *refs):
    out_ref = refs[-1]
    rows = refs[0].shape[2]
    half = out_ref.shape[2] // 2
    for u in range(2):
        for hops, piece in zip((0, SIDE - 1, 1, 2), refs[4 * u : 4 * u + 4]):
            start = u * half + lax.rem(place_ref[u] + hops, SIDE) * rows
            out_ref[:, :, pl.ds(pl.multiple_of(start, rows), rows), :] = piece[...]


def lay_activations(place, pieces):
    chips, layers, rows, width = pieces[0].shape
    shape = (chips, layers, 2 * SIDE * rows, width)
    return pl.pallas_call(
        lay_kernel,
        in_specs=[pl.BlockSpec(memory_space=pltpu.SMEM)]
        + [pl.BlockSpec(memory_space=pltpu.VMEM)] * len(pieces),
        out_specs=pl.BlockSpec(memory_space=pltpu.VMEM),
        out_shape=jax.ShapeDtypeStruct(shape, pieces[0].dtype),
        compiler_params=pltpu.CompilerParams(vmem_limit_bytes=14 * MIB),
        cost_estimate=pl.CostEstimate(
            flops=0, bytes_accessed=16 * 2 * SIDE * pieces[0].size, transcendentals=0
        ),
        name="lay_activations",
    )(place, *pieces)


def partial_kernel(core_ref, act_ref, *refs):
    parts, (kept_ref, given_ref) = refs[:-2], refs[-2:]
    holders, rows, tokens = parts[0].shape
    width = kept_ref.shape[-1]
    flat = [part[...].reshape(holders * rows, tokens) for part in parts]
    for out_ref, which in ((kept_ref, core_ref[0]), (given_ref, 1 - core_ref[0])):
        columns = pl.ds(pl.multiple_of(which * width, width), width)
        total = dot(flat[0], act_ref[0, 0, :, columns], NN)
        for n in range(1, len(flat)):
            total += dot(flat[n], act_ref[n, 0, :, columns], NN)
        out_ref[...] = total.astype(out_ref.dtype).reshape(out_ref.shape)


def gradient_partials(core, acts, parts):
    chips, layers, tokens, width = acts.shape
    holders, all_rows, _ = parts[0].shape
    rows, size = all_rows // layers, width // CORES
    shape = jax.ShapeDtypeStruct((holders, all_rows, size), acts.dtype)
    return pl.pallas_call(
        partial_kernel,
        grid_spec=pltpu.PrefetchScalarGridSpec(
            num_scalar_prefetch=1,
            grid=(layers, 2),
            in_specs=[pl.BlockSpec((chips, 1, tokens, width), lambda l, h, s: (0, l, 0, 0))]
            + [pl.BlockSpec((holders // 2, rows, tokens), lambda l, h, s: (h, l, 0))] * len(parts),
            out_specs=[pl.BlockSpec((holders // 2, rows, size), lambda l, h, s: (h, l, 0))] * 2,
        ),
        out_shape=[shape, shape],
        compiler_params=pltpu.CompilerParams(vmem_limit_bytes=24 * MIB),
        cost_estimate=pl.CostEstimate(
            flops=2 * holders * all_rows * chips * tokens * width,
            bytes_accessed=2 * (acts.size + chips * parts[0].size + 2 * holders * all_rows * size),
            transcendentals=0,
        ),
        name="gradient_partials",
    )(core, acts, *parts)


def deal_kernel(slot_ref, kept_ref, got_ref, out_ref):
    layer, half = pl.program_id(0), pl.program_id(1)
    holders, rows, _ = kept_ref.shape
    piece = out_ref.shape[1]
    cols = rows // piece
    for holder in range(holders):
        total = kept_ref[holder].astype(jnp.float32) + got_ref[holder].astype(jnp.float32)
        total = total.astype(out_ref.dtype)
        for col in range(cols):
            slot = slot_ref[((half * holders + holder) * 2 + layer) * cols + col]
            out_ref[slot] = total[col * piece : (col + 1) * piece]


def deal_to_slots(slots, kept, got, slot_total):
    holders, all_rows, size = kept.shape
    layers = 2
    rows = all_rows // layers
    shape = (holders * slot_total, TABLE_ROWS, size)
    return pl.pallas_call(
        deal_kernel,
        grid_spec=pltpu.PrefetchScalarGridSpec(
            num_scalar_prefetch=1,
            grid=(layers, 2),
            in_specs=[pl.BlockSpec((holders // 2, rows, size), lambda l, h, s: (h, l, 0))] * 2,
            out_specs=pl.BlockSpec(shape, lambda l, h, s: (0, 0, 0)),
        ),
        out_shape=jax.ShapeDtypeStruct(shape, kept.dtype),
        compiler_params=pltpu.CompilerParams(vmem_limit_bytes=16 * MIB),
        cost_estimate=pl.CostEstimate(
            flops=kept.size, bytes_accessed=8 * kept.size, transcendentals=0
        ),
        name="deal_to_slots",
    )(slots, kept, got)


def turned_block(slice_refs):
    width = slice_refs[0].shape[-1]
    return jnp.concatenate([ref[...].reshape(-1, width) for ref in slice_refs], axis=0)


def slot_kernel(source_ref, count_ref, left_ref, right_ref, *refs):
    slice_refs, (out_ref, left_stat_ref, right_stat_ref) = refs[:-3], refs[-3:]
    is_live = pl.program_id(0) < count_ref[0]

    @pl.when(is_live)
    def _():
        turned = turned_block(slice_refs)
        inner = dot(left_ref[0], turned, NT).astype(out_ref.dtype)
        out_ref[0] = dot(inner, right_ref[0], NN).astype(out_ref.dtype)
        scale = 1.0 / turned.shape[0]
        left_stat_ref[0] = (dot(turned, turned, TN) * scale).astype(left_stat_ref.dtype)
        right_stat_ref[0] = (dot(turned, turned, NT) * scale).astype(right_stat_ref.dtype)

    @pl.when(jnp.logical_not(is_live))
    def _():
        left_stat_ref[...] = jnp.zeros_like(left_stat_ref)
        right_stat_ref[...] = jnp.zeros_like(right_stat_ref)


def work_on_slots(sources, counts, left_roots, right_roots, arrived, owner_total):
    slot_total, size, _ = left_roots.shape

    def out_place(s, source, count):
        return (source[jnp.minimum(s, count[0] - 1)], 0, 0)

    def live(s, source, count):
        return (s, 0, 0)

    def slice_spec(a):
        return pl.BlockSpec((a.shape[0], 1) + a.shape[2:], lambda s, *_: (0, s, 0, 0))

    stats = jax.ShapeDtypeStruct((slot_total, size, size), left_roots.dtype)
    return pl.pallas_call(
        slot_kernel,
        grid_spec=pltpu.PrefetchScalarGridSpec(
            num_scalar_prefetch=2,
            grid=(slot_total,),
            in_specs=[pl.BlockSpec((1, size, size), live)] * 2 + [slice_spec(a) for a in arrived],
            out_specs=[
                pl.BlockSpec((1, size, size), out_place),
                pl.BlockSpec((1, size, size), live),
                pl.BlockSpec((1, size, size), live),
            ],
        ),
        out_shape=[jax.ShapeDtypeStruct((owner_total, size, size), left_roots.dtype), stats, stats],
        compiler_params=pltpu.CompilerParams(vmem_limit_bytes=24 * MIB),
        cost_estimate=pl.CostEstimate(
            flops=8 * slot_total * size**3,
            bytes_accessed=12 * slot_total * size * size,
            transcendentals=0,
        ),
        name="work_on_slots",
    )(sources, counts, left_roots, right_roots, *arrived)


def place_kernel(owner_ref, returned_ref, out_ref, held, in_sems, out_sems):
    layers, size, width = out_ref.shape
    cols = width // size
    blocks = [(l, c, l * cols + c) for l in range(layers) for c in range(cols)]
    fetches = [
        pltpu.make_async_copy(returned_ref.at[owner_ref[t]], held.at[t], in_sems.at[t])
        for _, _, t in blocks
    ]
    stores = [
        pltpu.make_async_copy(
            held.at[t], out_ref.at[l, :, pl.ds(c * size, size)], out_sems.at[t]
        )
        for l, c, t in blocks
    ]
    for fetch in fetches:
        fetch.start()
    for fetch, store in zip(fetches, stores):
        fetch.wait()
        store.start()
    for store in stores:
        store.wait()


def place_blocks(owners, returned, layers, cols):
    _, size, _ = returned.shape
    return pl.pallas_call(
        place_kernel,
        in_specs=[
            pl.BlockSpec(memory_space=pltpu.SMEM),
            pl.BlockSpec(memory_space=pl.ANY),
        ],
        out_specs=pl.BlockSpec(memory_space=pl.ANY),
        out_shape=jax.ShapeDtypeStruct((layers, size, cols * size), returned.dtype),
        scratch_shapes=[
            pltpu.VMEM((layers * cols, size, size), returned.dtype),
            pltpu.SemaphoreType.DMA((layers * cols,)),
            pltpu.SemaphoreType.DMA((layers * cols,)),
        ],
        compiler_params=pltpu.CompilerParams(vmem_limit_bytes=8 * MIB),
        cost_estimate=pl.CostEstimate(
            flops=0, bytes_accessed=4 * layers * cols * size * size, transcendentals=0
        ),
        name="place_blocks",
    )(owners, returned)


def activations_for_chips(activations, chip_y, place):
    layers, tokens, width = activations.shape
    rows = tokens // 2 // SIDE
    pair_width = width // SIDE
    mine = jnp.stack(
        [
            lax.dynamic_slice(
                activations, (0, u * (tokens // 2) + place[u] * rows, 0), (layers, rows, width)
            )
            for u in range(2)
        ]
    )
    return [
        lax.dynamic_slice(
            mine,
            (0, 0, 0, lax.rem(chip_y + hops, SIDE) * pair_width),
            mine.shape[:3] + (pair_width,),
        )
        for hops in (0, 1, SIDE - 1, 2)
    ]


def on_device(
    activations, cotangents, left_root, right_root, block_owner, owned_sources, owner_counts
):
    owner_total = lax.axis_size("mp")
    layers, _, width = cotangents.shape
    slot_total, size = left_root.shape[2], left_root.shape[-1]
    cols = width // size
    blocks = layers * cols
    owners = block_owner.reshape(-1)
    group, holder = lax.axis_index("dp"), lax.axis_index("mp")
    chip_y, core = group // CORES, lax.rem(group, CORES)
    place = (lax.rem(holder, SIDE), holder // SIDE)

    for_chips = activations_for_chips(activations, chip_y, place)
    from_chips = [for_chips[0]] + [
        along_y(piece, hops) for piece, hops in zip(for_chips[1:], (1, -1, 2))
    ]
    spread = exchange(split_cotangents(owners, after(cotangents, *for_chips), owner_total))
    base = spread.shape[1] - TABLE_ROWS
    chunk = base // CHUNKS

    own_piece = after(from_chips[0], spread)
    halves = [jnp.stack([own_piece[u]] + [piece[u] for piece in from_chips[1:]]) for u in range(2)]
    first_parts = ring(spread[:, :chunk], along_y)
    pieces = ring(halves[0], along_z) + ring(halves[1], along_x)
    moved = lax.optimization_barrier(first_parts + pieces)
    first_parts, pieces = moved[:SIDE], moved[SIDE:]
    acts = lay_activations(jnp.stack(place).astype(jnp.int32), pieces)
    second_parts = ring(after(spread[:, chunk:base], *first_parts), along_y)

    owner_of = spread[:, base : base + blocks, 0].astype(jnp.int32)
    all_owners = jnp.arange(owner_total, dtype=jnp.int32)
    named = (owner_of[:, :, None] == all_owners).astype(jnp.int32)
    given = jnp.sum(named, axis=1)
    earlier = (all_owners[:, None] > all_owners[None, :]).astype(jnp.int32)
    slot_of = jnp.sum(earlier[:, :, None] * given[None, :, :], axis=1)
    slots = (owner_of * slot_total + jnp.sum(named * slot_of[:, None, :], axis=-1)).reshape(-1)

    def sliced_slots(core, parts):
        kept, given = gradient_partials(core, acts, parts)
        return exchange(deal_to_slots(slots, kept, other_core(given), slot_total))

    core = core.reshape(1).astype(jnp.int32)
    arrived = sliced_slots(after(core, slots), first_parts)
    more = sliced_slots(after(core, arrived), second_parts)

    def by_slot(value):
        return value.reshape((owner_total, slot_total) + value.shape[1:])

    returning, left_stats, right_stats = work_on_slots(
        owned_sources.reshape(-1),
        owner_counts.reshape(-1),
        left_root.reshape(slot_total, size, size),
        right_root.reshape(slot_total, size, size),
        (by_slot(arrived), by_slot(more)),
        owner_total,
    )
    precond = place_blocks(owners, exchange(returning), layers, cols)
    stat_shape = (1, 1, slot_total, size, size)
    return (precond, left_stats.reshape(stat_shape), right_stats.reshape(stat_shape))


def solution(mesh):
    placed = (
        P(None, "dp", None),
        P(None, "dp", "mp"),
        P("dp", "mp", None, None, None),
        P("dp", "mp", None, None, None),
        P("dp", "mp", None),
        P("dp", "mp", None),
        P("dp", "mp"),
    )
    return jax.shard_map(
        on_device,
        mesh=mesh,
        in_specs=placed,
        out_specs=(
            P(None, "dp", "mp"),
            P("dp", "mp", None, None, None),
            P("dp", "mp", None, None, None),
        ),
        check_vma=False,
    )
```

```python
import functools

import jax
import jax.numpy as jnp
from jax import lax
from jax.experimental import pallas as pl
from jax.experimental.pallas import tpu as pltpu
from jax.sharding import PartitionSpec as P

CHUNKS = 2
SIDE = 4
CORES = 2
TABLE_ROWS = 16
MIB = 1024 * 1024

NT = (((1,), (1,)), ((), ()))
NN = (((1,), (0,)), ((), ()))
TN = (((0,), (0,)), ((), ()))


def dot(a, b, dims):
    return lax.dot_general(a, b, dims, preferred_element_type=jnp.float32)


def along_y(value, hops):
    pairs = [
        (y * CORES + c, (y + hops) % SIDE * CORES + c) for y in range(SIDE) for c in range(CORES)
    ]
    return lax.ppermute(value, "dp", pairs)


def other_core(value):
    pairs = [(y * CORES + c, y * CORES + 1 - c) for y in range(SIDE) for c in range(CORES)]
    return lax.ppermute(value, "dp", pairs)


def along_z(value, hops):
    pairs = [(x * SIDE + z, x * SIDE + (z + hops) % SIDE) for x in range(SIDE) for z in range(SIDE)]
    return lax.ppermute(value, "mp", pairs)


def ring_in_two(value, move):
    half = value.shape[0] // 2
    before, behind = move(value, 1), move(value, -1)
    return (value, before, behind, move(before[:half], 1), move(behind[half:], -1))


def exchange(value):
    return lax.all_to_all(value, "mp", split_axis=0, concat_axis=0, tiled=True)


def after(value, *needed):
    return lax.optimization_barrier((value,) + needed)[0]


def split_kernel(owner_ref, cot_ref, out_ref):
    layers, tokens, width = cot_ref.shape
    parts, piece = out_ref.shape[0], TABLE_ROWS
    size = parts * piece * CHUNKS
    cols = width // size
    for layer in range(layers):
        for col in range(cols):
            turned = cot_ref[layer, :, col * size : (col + 1) * size].T
            for q in range(CHUNKS):
                row = ((q * layers + layer) * cols + col) * piece
                half = turned[q * parts * piece : (q + 1) * parts * piece]
                out_ref[:, row : row + piece, :] = half.reshape(parts, piece, tokens)
    rows = lax.broadcasted_iota(jnp.int32, (TABLE_ROWS, tokens), 0)
    table = jnp.zeros((TABLE_ROWS, tokens), jnp.float32)
    for t in range(layers * cols):
        table = jnp.where(rows == t, owner_ref[t].astype(jnp.float32), table)
    base = CHUNKS * layers * cols * piece
    for part in range(parts):
        out_ref[part, base : base + TABLE_ROWS, :] = table.astype(out_ref.dtype)


def split_cotangents(owners, cotangents, owner_total):
    layers, tokens, width = cotangents.shape
    rows = width * layers // owner_total
    return pl.pallas_call(
        split_kernel,
        in_specs=[
            pl.BlockSpec(memory_space=pltpu.SMEM),
            pl.BlockSpec(memory_space=pltpu.VMEM),
        ],
        out_specs=pl.BlockSpec(memory_space=pltpu.VMEM),
        out_shape=jax.ShapeDtypeStruct((owner_total, rows + TABLE_ROWS, tokens), cotangents.dtype),
        compiler_params=pltpu.CompilerParams(vmem_limit_bytes=6 * MIB),
        cost_estimate=pl.CostEstimate(
            flops=0, bytes_accessed=4 * cotangents.size, transcendentals=0
        ),
        name="split_cotangents",
    )(owners, cotangents)


def partial_kernel(here_ref, *refs):
    pieces, parts, (kept_ref, given_ref, acts, held, sems) = refs[:4], refs[4:-5], refs[-5:]
    _, layers, count, _ = pieces[0].shape
    _, holders, all_rows, tokens = held.shape
    width = kept_ref.shape[-1]
    rows, half = all_rows // layers, holders // 2

    def fetches(layer):
        moves = []
        for n, part in enumerate(parts):
            to = held.at[min(n, 3)]
            if part.shape[0] == half:
                to = to.at[pl.ds((n - 3) * half, half)]
            mine = pl.ds(layer * rows, rows)
            moves.append((part.at[:, mine, :], to.at[:, mine, :]))
        for n, piece in enumerate(pieces):
            first = here_ref[1] if n < 2 else 1 - here_ref[1]
            start = pl.multiple_of((first * 2 + n % 2) * count, count)
            moves.append((piece.at[:, layer], acts.at[layer, :, pl.ds(start, count), :]))
        return [pltpu.make_async_copy(*move, sems.at[layer, n]) for n, move in enumerate(moves)]

    for layer in range(layers):
        for fetch in fetches(layer):
            fetch.start()
    for layer in range(layers):
        for fetch in fetches(layer):
            fetch.wait()
        mine = slice(layer * rows, (layer + 1) * rows)
        for side in range(2):
            some = slice(side * half, (side + 1) * half)
            flat = [held[n, some, mine, :].reshape(half * rows, tokens) for n in range(4)]
            for out_ref, which in ((kept_ref, here_ref[0]), (given_ref, 1 - here_ref[0])):
                columns = pl.ds(pl.multiple_of(which * width, width), width)
                total = dot(flat[0], acts[layer, 0, :, columns], NN)
                for n in range(1, SIDE):
                    total += dot(flat[n], acts[layer, n, :, columns], NN)
                out_ref[some, mine, :] = total.astype(out_ref.dtype).reshape(half, rows, width)


def gradient_partials(here, pieces, parts):
    chips, layers, _, width = pieces[0].shape
    holders, all_rows, tokens = parts[0].shape
    kind = parts[0].dtype
    shape = jax.ShapeDtypeStruct((holders, all_rows, width // CORES), kind)
    inputs = len(pieces) + len(parts)
    return pl.pallas_call(
        partial_kernel,
        in_specs=[pl.BlockSpec(memory_space=pltpu.SMEM)]
        + [pl.BlockSpec(memory_space=pl.ANY)] * inputs,
        out_specs=[pl.BlockSpec(memory_space=pltpu.VMEM)] * 2,
        scratch_shapes=[
            pltpu.VMEM((layers, chips, tokens, width), kind),
            pltpu.VMEM((SIDE, holders, all_rows, tokens), kind),
            pltpu.SemaphoreType.DMA((layers, inputs)),
        ],
        out_shape=[shape, shape],
        compiler_params=pltpu.CompilerParams(vmem_limit_bytes=50 * MIB),
        cost_estimate=pl.CostEstimate(flops=0, bytes_accessed=1024, transcendentals=0),
        name="gradient_partials",
    )(here, *pieces, *parts)


def deal_kernel(slot_ref, kept_ref, got_ref, out_ref):
    layer, half = pl.program_id(0), pl.program_id(1)
    holders, rows, _ = kept_ref.shape
    piece = out_ref.shape[1]
    cols = rows // piece
    for holder in range(holders):
        total = kept_ref[holder].astype(jnp.float32) + got_ref[holder].astype(jnp.float32)
        total = total.astype(out_ref.dtype)
        for col in range(cols):
            slot = slot_ref[((half * holders + holder) * 2 + layer) * cols + col]
            out_ref[slot] = total[col * piece : (col + 1) * piece]


def deal_to_slots(slots, kept, got, slot_total):
    holders, all_rows, size = kept.shape
    layers = 2
    rows = all_rows // layers
    shape = (holders * slot_total, TABLE_ROWS, size)
    return pl.pallas_call(
        deal_kernel,
        grid_spec=pltpu.PrefetchScalarGridSpec(
            num_scalar_prefetch=1,
            grid=(layers, 2),
            in_specs=[pl.BlockSpec((holders // 2, rows, size), lambda l, h, s: (h, l, 0))] * 2,
            out_specs=pl.BlockSpec(shape, lambda l, h, s: (0, 0, 0)),
        ),
        out_shape=jax.ShapeDtypeStruct(shape, kept.dtype),
        compiler_params=pltpu.CompilerParams(vmem_limit_bytes=6 * MIB),
        cost_estimate=pl.CostEstimate(flops=0, bytes_accessed=1024, transcendentals=0),
        name="deal_to_slots",
    )(slots, kept, got)


def slot_kernel(source_ref, left_ref, right_ref, first_ref, second_ref, *refs):
    out_ref, left_stat_ref, right_stat_ref, lefts, rights, turns, sems = refs
    slot = pl.program_id(0)
    slot_total, size, _ = lefts.shape

    def fetches(s):
        moves = [(left_ref.at[s], lefts.at[s]), (right_ref.at[s], rights.at[s])]
        moves += [(ref.at[:, s], turns.at[s, q]) for q, ref in enumerate((first_ref, second_ref))]
        return [pltpu.make_async_copy(*move, sems.at[s, n]) for n, move in enumerate(moves)]

    @pl.when(slot == 0)
    def _():
        for s in range(slot_total):
            for fetch in fetches(s):
                fetch.start()

    for fetch in fetches(slot):
        fetch.wait()
    is_live = source_ref[slot] >= 0

    @pl.when(is_live)
    def _():
        turned = turns[slot].reshape(size, size)
        inner = dot(lefts[slot], turned, NT).astype(out_ref.dtype)
        out_ref[0] = dot(inner, rights[slot], NN).astype(out_ref.dtype)
        scale = 1.0 / size
        left_stat_ref[0] = (dot(turned, turned, TN) * scale).astype(left_stat_ref.dtype)
        right_stat_ref[0] = (dot(turned, turned, NT) * scale).astype(right_stat_ref.dtype)

    @pl.when(jnp.logical_not(is_live))
    def _():
        left_stat_ref[...] = jnp.zeros_like(left_stat_ref)
        right_stat_ref[...] = jnp.zeros_like(right_stat_ref)


def work_on_slots(sources, left_roots, right_roots, arrived, owner_total):
    slot_total, size, _ = left_roots.shape
    kind = left_roots.dtype
    slices = arrived[0].shape

    def out_place(s, source):
        place = source[s]
        for back in range(1, slot_total):
            place = jnp.where(place >= 0, place, source[jnp.maximum(s - back, 0)])
        return (place, 0, 0)

    def live(s, source):
        return (s, 0, 0)

    stats = jax.ShapeDtypeStruct((slot_total, size, size), kind)
    return pl.pallas_call(
        slot_kernel,
        grid_spec=pltpu.PrefetchScalarGridSpec(
            num_scalar_prefetch=1,
            grid=(slot_total,),
            in_specs=[pl.BlockSpec(memory_space=pl.ANY)] * 4,
            out_specs=[
                pl.BlockSpec((1, size, size), out_place),
                pl.BlockSpec((1, size, size), live),
                pl.BlockSpec((1, size, size), live),
            ],
            scratch_shapes=[
                pltpu.VMEM((slot_total, size, size), kind),
                pltpu.VMEM((slot_total, size, size), kind),
                pltpu.VMEM((slot_total, CHUNKS, slices[0], slices[2], size), kind),
                pltpu.SemaphoreType.DMA((slot_total, 4)),
            ],
        ),
        out_shape=[jax.ShapeDtypeStruct((owner_total, size, size), kind), stats, stats],
        compiler_params=pltpu.CompilerParams(vmem_limit_bytes=50 * MIB),
        cost_estimate=pl.CostEstimate(
            flops=8 * slot_total * size**3,
            bytes_accessed=12 * slot_total * size * size,
            transcendentals=0,
        ),
        name="work_on_slots",
    )(sources, left_roots, right_roots, *arrived)


def place_kernel(owner_ref, returned_ref, out_ref, held, in_sems, out_sems):
    layers, size, width = out_ref.shape
    cols = width // size
    blocks = [(l, c, l * cols + c) for l in range(layers) for c in range(cols)]
    fetches = [
        pltpu.make_async_copy(returned_ref.at[owner_ref[t]], held.at[t], in_sems.at[t])
        for _, _, t in blocks
    ]
    stores = [
        pltpu.make_async_copy(
            held.at[t], out_ref.at[l, :, pl.ds(c * size, size)], out_sems.at[t]
        )
        for l, c, t in blocks
    ]
    for fetch in fetches:
        fetch.start()
    for fetch, store in zip(fetches, stores):
        fetch.wait()
        store.start()
    for store in stores:
        store.wait()


def place_blocks(owners, returned, layers, cols):
    _, size, _ = returned.shape
    return pl.pallas_call(
        place_kernel,
        in_specs=[
            pl.BlockSpec(memory_space=pltpu.SMEM),
            pl.BlockSpec(memory_space=pl.ANY),
        ],
        out_specs=pl.BlockSpec(memory_space=pl.ANY),
        out_shape=jax.ShapeDtypeStruct((layers, size, cols * size), returned.dtype),
        scratch_shapes=[
            pltpu.VMEM((layers * cols, size, size), returned.dtype),
            pltpu.SemaphoreType.DMA((layers * cols,)),
            pltpu.SemaphoreType.DMA((layers * cols,)),
        ],
        compiler_params=pltpu.CompilerParams(vmem_limit_bytes=8 * MIB),
        cost_estimate=pl.CostEstimate(
            flops=0, bytes_accessed=4 * layers * cols * size * size, transcendentals=0
        ),
        name="place_blocks",
    )(owners, returned)


def activations_for_chips(activations, chip_y, parity):
    layers, tokens, width = activations.shape
    rows, pair_width = tokens // 4, width // SIDE
    return [
        jnp.stack(
            [
                lax.dynamic_slice(
                    activations,
                    (0, (parity * 2 + u) * rows, lax.rem(chip_y + hops, SIDE) * pair_width),
                    (layers, rows, pair_width),
                )
                for u in range(2)
            ]
        )
        for hops in (0, 1, SIDE - 1, 2)
    ]


def on_device(
    activations, cotangents, left_root, right_root, block_owner, owned_sources, owner_counts
):
    owner_total = lax.axis_size("mp")
    layers, _, width = cotangents.shape
    slot_total, size = left_root.shape[2], left_root.shape[-1]
    cols = width // size
    blocks = layers * cols
    owners = block_owner.reshape(-1)
    group, holder = lax.axis_index("dp"), lax.axis_index("mp")
    chip_y, core = group // CORES, lax.rem(group, CORES)
    parity = lax.rem(holder, 2)

    split = split_cotangents(owners, cotangents, owner_total)
    spread = exchange(split)
    for_chips = activations_for_chips(after(activations, split), chip_y, parity)
    from_chips = [for_chips[0]] + [
        along_y(piece, hops) for piece, hops in zip(for_chips[1:], (1, -1, 2))
    ]
    base = spread.shape[1] - TABLE_ROWS
    chunk = base // CHUNKS

    halves = [jnp.stack([piece[u] for piece in from_chips]) for u in range(2)]
    first_parts = ring_in_two(spread[:, :chunk], along_y)
    pieces = (halves[0], halves[1], along_z(halves[0], 1), along_z(halves[1], -1))
    second = after(spread[:, chunk:base], *first_parts)
    second_parts = (second, along_y(second, 1), along_y(second, -1), along_y(second, 2))

    owner_of = spread[:, base : base + blocks, 0].astype(jnp.int32)
    all_owners = jnp.arange(owner_total, dtype=jnp.int32)
    named = (owner_of[:, :, None] == all_owners).astype(jnp.int32)
    given = jnp.sum(named, axis=1)
    earlier = (all_owners[:, None] > all_owners[None, :]).astype(jnp.int32)
    slot_of = jnp.sum(earlier[:, :, None] * given[None, :, :], axis=1)
    slots = (owner_of * slot_total + jnp.sum(named * slot_of[:, None, :], axis=-1)).reshape(-1)

    def sliced_slots(here, parts):
        kept, given = gradient_partials(here, pieces, parts)
        return deal_to_slots(slots, kept, other_core(given), slot_total)

    slot_range = jnp.arange(slot_total, dtype=jnp.int32)
    sources = jnp.where(slot_range < owner_counts.reshape(()), owned_sources.reshape(-1), -1)
    here = jnp.stack((core, parity)).astype(jnp.int32)
    here, slots, sources = lax.optimization_barrier((here, slots, sources))
    dealt = sliced_slots(here, first_parts)
    arrived = exchange(dealt)
    dealt = sliced_slots(after(here, dealt), second_parts)
    dealt, arrived = lax.optimization_barrier((dealt, arrived))
    more = exchange(dealt)

    def by_slot(value):
        return value.reshape((owner_total, slot_total) + value.shape[1:])

    returning, left_stats, right_stats = work_on_slots(
        sources,
        left_root.reshape(slot_total, size, size),
        right_root.reshape(slot_total, size, size),
        (by_slot(arrived), by_slot(more)),
        owner_total,
    )
    precond = place_blocks(owners, exchange(returning), layers, cols)
    stat_shape = (1, 1, slot_total, size, size)
    return (precond, left_stats.reshape(stat_shape), right_stats.reshape(stat_shape))


def solution(mesh):
    placed = (
        P(None, "dp", None),
        P(None, "dp", "mp"),
        P("dp", "mp", None, None, None),
        P("dp", "mp", None, None, None),
        P("dp", "mp", None),
        P("dp", "mp", None),
        P("dp", "mp"),
    )
    return jax.shard_map(
        on_device,
        mesh=mesh,
        in_specs=placed,
        out_specs=(
            P(None, "dp", "mp"),
            P("dp", "mp", None, None, None),
            P("dp", "mp", None, None, None),
        ),
        check_vma=False,
    )
```

```python
import functools

import jax
import jax.numpy as jnp
from jax import lax
from jax.experimental import pallas as pl
from jax.experimental.pallas import tpu as pltpu
from jax.sharding import PartitionSpec as P

CHUNKS = 2
SIDE = 4
CORES = 2
TABLE_ROWS = 16
MIB = 1024 * 1024

NT = (((1,), (1,)), ((), ()))
NN = (((1,), (0,)), ((), ()))
TN = (((0,), (0,)), ((), ()))


def dot(a, b, dims):
    return lax.dot_general(a, b, dims, preferred_element_type=jnp.float32)


def along_y(value, hops):
    pairs = [
        (y * CORES + c, (y + hops) % SIDE * CORES + c) for y in range(SIDE) for c in range(CORES)
    ]
    return lax.ppermute(value, "dp", pairs)


def other_core(value):
    pairs = [(y * CORES + c, y * CORES + 1 - c) for y in range(SIDE) for c in range(CORES)]
    return lax.ppermute(value, "dp", pairs)


def along_z(value, hops):
    pairs = [(x * SIDE + z, x * SIDE + (z + hops) % SIDE) for x in range(SIDE) for z in range(SIDE)]
    return lax.ppermute(value, "mp", pairs)


def ring_in_two(value, move):
    half = value.shape[0] // 2
    before, behind = move(value, 1), move(value, -1)
    return (value, before, behind, move(before[:half], 1), move(behind[half:], -1))


def exchange(value):
    return lax.all_to_all(value, "mp", split_axis=0, concat_axis=0, tiled=True)


def after(value, *needed):
    return lax.optimization_barrier((value,) + needed)[0]


def split_kernel(owner_ref, cot_ref, *out_refs):
    layers, tokens, width = cot_ref.shape
    parts, piece = out_refs[0].shape[0], TABLE_ROWS
    size = parts * piece * CHUNKS
    cols = width // size
    for layer in range(layers):
        for col in range(cols):
            turned = cot_ref[layer, :, col * size : (col + 1) * size].T
            row = (layer * cols + col) * piece
            for q, out_ref in enumerate(out_refs):
                half = turned[q * parts * piece : (q + 1) * parts * piece]
                out_ref[:, row : row + piece, :] = half.reshape(parts, piece, tokens)
    rows = lax.broadcasted_iota(jnp.int32, (TABLE_ROWS, tokens), 0)
    table = jnp.zeros((TABLE_ROWS, tokens), jnp.float32)
    for t in range(layers * cols):
        table = jnp.where(rows == t, owner_ref[t].astype(jnp.float32), table)
    base, out_ref = layers * cols * piece, out_refs[-1]
    for part in range(parts):
        out_ref[part, base : base + TABLE_ROWS, :] = table.astype(out_ref.dtype)


def split_cotangents(owners, cotangents, owner_total):
    layers, tokens, width = cotangents.shape
    rows = width * layers // owner_total // CHUNKS
    return pl.pallas_call(
        split_kernel,
        in_specs=[
            pl.BlockSpec(memory_space=pltpu.SMEM),
            pl.BlockSpec(memory_space=pltpu.VMEM),
        ],
        out_specs=[pl.BlockSpec(memory_space=pltpu.VMEM)] * 2,
        out_shape=[
            jax.ShapeDtypeStruct((owner_total, rows, tokens), cotangents.dtype),
            jax.ShapeDtypeStruct((owner_total, rows + TABLE_ROWS, tokens), cotangents.dtype),
        ],
        compiler_params=pltpu.CompilerParams(vmem_limit_bytes=6 * MIB),
        cost_estimate=pl.CostEstimate(
            flops=0, bytes_accessed=4 * cotangents.size, transcendentals=0
        ),
        name="split_cotangents",
    )(owners, cotangents)


def partial_kernel(here_ref, *refs):
    pieces, parts, (kept_ref, given_ref, acts, held, sems) = refs[:4], refs[4:-5], refs[-5:]
    _, layers, count, _ = pieces[0].shape
    _, holders, all_rows, tokens = held.shape
    width = kept_ref.shape[-1]
    rows, half = all_rows // layers, holders // 2

    def fetches(layer):
        moves = []
        for n, part in enumerate(parts):
            to = held.at[min(n, 3)]
            if part.shape[0] == half:
                to = to.at[pl.ds((n - 3) * half, half)]
            mine = pl.ds(layer * rows, rows)
            moves.append((part.at[:, mine, :], to.at[:, mine, :]))
        for n, piece in enumerate(pieces):
            first = here_ref[1] if n < 2 else 1 - here_ref[1]
            start = pl.multiple_of((first * 2 + n % 2) * count, count)
            moves.append((piece.at[:, layer], acts.at[layer, :, pl.ds(start, count), :]))
        return [pltpu.make_async_copy(*move, sems.at[layer, n]) for n, move in enumerate(moves)]

    for layer in range(layers):
        for fetch in fetches(layer):
            fetch.start()
    for layer in range(layers):
        for fetch in fetches(layer):
            fetch.wait()
        mine = slice(layer * rows, (layer + 1) * rows)
        for side in range(2):
            some = slice(side * half, (side + 1) * half)
            flat = [held[n, some, mine, :].reshape(half * rows, tokens) for n in range(4)]
            for out_ref, which in ((kept_ref, here_ref[0]), (given_ref, 1 - here_ref[0])):
                columns = pl.ds(pl.multiple_of(which * width, width), width)
                total = dot(flat[0], acts[layer, 0, :, columns], NN)
                for n in range(1, SIDE):
                    total += dot(flat[n], acts[layer, n, :, columns], NN)
                out_ref[some, mine, :] = total.astype(out_ref.dtype).reshape(half, rows, width)


def gradient_partials(here, pieces, parts):
    chips, layers, _, width = pieces[0].shape
    holders, all_rows, tokens = parts[0].shape
    kind = parts[0].dtype
    shape = jax.ShapeDtypeStruct((holders, all_rows, width // CORES), kind)
    inputs = len(pieces) + len(parts)
    return pl.pallas_call(
        partial_kernel,
        in_specs=[pl.BlockSpec(memory_space=pltpu.SMEM)]
        + [pl.BlockSpec(memory_space=pl.ANY)] * inputs,
        out_specs=[pl.BlockSpec(memory_space=pltpu.VMEM)] * 2,
        scratch_shapes=[
            pltpu.VMEM((layers, chips, tokens, width), kind),
            pltpu.VMEM((SIDE, holders, all_rows, tokens), kind),
            pltpu.SemaphoreType.DMA((layers, inputs)),
        ],
        out_shape=[shape, shape],
        compiler_params=pltpu.CompilerParams(vmem_limit_bytes=50 * MIB),
        cost_estimate=pl.CostEstimate(flops=0, bytes_accessed=1024, transcendentals=0),
        name="gradient_partials",
    )(here, *pieces, *parts)


def deal_kernel(slot_ref, kept_ref, got_ref, out_ref):
    layer, half = pl.program_id(0), pl.program_id(1)
    holders, rows, _ = kept_ref.shape
    piece = out_ref.shape[1]
    cols = rows // piece
    for holder in range(holders):
        total = kept_ref[holder].astype(jnp.float32) + got_ref[holder].astype(jnp.float32)
        total = total.astype(out_ref.dtype)
        for col in range(cols):
            slot = slot_ref[((half * holders + holder) * 2 + layer) * cols + col]
            out_ref[slot] = total[col * piece : (col + 1) * piece]


def deal_to_slots(slots, kept, got, slot_total):
    holders, all_rows, size = kept.shape
    layers = 2
    rows = all_rows // layers
    shape = (holders * slot_total, TABLE_ROWS, size)
    return pl.pallas_call(
        deal_kernel,
        grid_spec=pltpu.PrefetchScalarGridSpec(
            num_scalar_prefetch=1,
            grid=(layers, 2),
            in_specs=[pl.BlockSpec((holders // 2, rows, size), lambda l, h, s: (h, l, 0))] * 2,
            out_specs=pl.BlockSpec(shape, lambda l, h, s: (0, 0, 0)),
        ),
        out_shape=jax.ShapeDtypeStruct(shape, kept.dtype),
        compiler_params=pltpu.CompilerParams(vmem_limit_bytes=6 * MIB),
        cost_estimate=pl.CostEstimate(flops=0, bytes_accessed=1024, transcendentals=0),
        name="deal_to_slots",
    )(slots, kept, got)


def slot_kernel(source_ref, left_ref, right_ref, first_ref, second_ref, *refs):
    out_ref, left_stat_ref, right_stat_ref, lefts, rights, turns, sems = refs
    slot = pl.program_id(0)
    slot_total, size, _ = lefts.shape

    def fetches(s):
        moves = [(left_ref.at[s], lefts.at[s]), (right_ref.at[s], rights.at[s])]
        moves += [(ref.at[:, s], turns.at[s, q]) for q, ref in enumerate((first_ref, second_ref))]
        return [pltpu.make_async_copy(*move, sems.at[s, n]) for n, move in enumerate(moves)]

    @pl.when(slot == 0)
    def _():
        for s in range(slot_total):
            for fetch in fetches(s):
                fetch.start()

    for fetch in fetches(slot):
        fetch.wait()
    is_live = source_ref[slot] >= 0

    @pl.when(is_live)
    def _():
        turned = turns[slot].reshape(size, size)
        inner = dot(lefts[slot], turned, NT).astype(out_ref.dtype)
        out_ref[0] = dot(inner, rights[slot], NN).astype(out_ref.dtype)
        scale = 1.0 / size
        left_stat_ref[0] = (dot(turned, turned, TN) * scale).astype(left_stat_ref.dtype)
        right_stat_ref[0] = (dot(turned, turned, NT) * scale).astype(right_stat_ref.dtype)

    @pl.when(jnp.logical_not(is_live))
    def _():
        left_stat_ref[...] = jnp.zeros_like(left_stat_ref)
        right_stat_ref[...] = jnp.zeros_like(right_stat_ref)


def work_on_slots(sources, left_roots, right_roots, arrived, owner_total):
    slot_total, size, _ = left_roots.shape
    kind = left_roots.dtype
    slices = arrived[0].shape

    def out_place(s, source):
        place = source[s]
        for back in range(1, slot_total):
            place = jnp.where(place >= 0, place, source[jnp.maximum(s - back, 0)])
        return (place, 0, 0)

    def live(s, source):
        return (s, 0, 0)

    stats = jax.ShapeDtypeStruct((slot_total, size, size), kind)
    return pl.pallas_call(
        slot_kernel,
        grid_spec=pltpu.PrefetchScalarGridSpec(
            num_scalar_prefetch=1,
            grid=(slot_total,),
            in_specs=[pl.BlockSpec(memory_space=pl.ANY)] * 4,
            out_specs=[
                pl.BlockSpec((1, size, size), out_place),
                pl.BlockSpec((1, size, size), live),
                pl.BlockSpec((1, size, size), live),
            ],
            scratch_shapes=[
                pltpu.VMEM((slot_total, size, size), kind),
                pltpu.VMEM((slot_total, size, size), kind),
                pltpu.VMEM((slot_total, CHUNKS, slices[0], slices[2], size), kind),
                pltpu.SemaphoreType.DMA((slot_total, 4)),
            ],
        ),
        out_shape=[jax.ShapeDtypeStruct((owner_total, size, size), kind), stats, stats],
        compiler_params=pltpu.CompilerParams(vmem_limit_bytes=50 * MIB),
        cost_estimate=pl.CostEstimate(
            flops=8 * slot_total * size**3,
            bytes_accessed=12 * slot_total * size * size,
            transcendentals=0,
        ),
        name="work_on_slots",
    )(sources, left_roots, right_roots, *arrived)


def place_kernel(owner_ref, returned_ref, out_ref, held, in_sems, out_sems):
    layers, size, width = out_ref.shape
    cols = width // size
    blocks = [(l, c, l * cols + c) for l in range(layers) for c in range(cols)]
    fetches = [
        pltpu.make_async_copy(returned_ref.at[owner_ref[t]], held.at[t], in_sems.at[t])
        for _, _, t in blocks
    ]
    stores = [
        pltpu.make_async_copy(
            held.at[t], out_ref.at[l, :, pl.ds(c * size, size)], out_sems.at[t]
        )
        for l, c, t in blocks
    ]
    for fetch in fetches:
        fetch.start()
    for fetch, store in zip(fetches, stores):
        fetch.wait()
        store.start()
    for store in stores:
        store.wait()


def place_blocks(owners, returned, layers, cols):
    _, size, _ = returned.shape
    return pl.pallas_call(
        place_kernel,
        in_specs=[
            pl.BlockSpec(memory_space=pltpu.SMEM),
            pl.BlockSpec(memory_space=pl.ANY),
        ],
        out_specs=pl.BlockSpec(memory_space=pl.ANY),
        out_shape=jax.ShapeDtypeStruct((layers, size, cols * size), returned.dtype),
        scratch_shapes=[
            pltpu.VMEM((layers * cols, size, size), returned.dtype),
            pltpu.SemaphoreType.DMA((layers * cols,)),
            pltpu.SemaphoreType.DMA((layers * cols,)),
        ],
        compiler_params=pltpu.CompilerParams(vmem_limit_bytes=8 * MIB),
        cost_estimate=pl.CostEstimate(
            flops=0, bytes_accessed=4 * layers * cols * size * size, transcendentals=0
        ),
        name="place_blocks",
    )(owners, returned)


def activations_for_chips(activations, chip_y, parity):
    layers, tokens, width = activations.shape
    rows, pair_width = tokens // 4, width // SIDE
    return [
        jnp.stack(
            [
                lax.dynamic_slice(
                    activations,
                    (0, (parity * 2 + u) * rows, lax.rem(chip_y + hops, SIDE) * pair_width),
                    (layers, rows, pair_width),
                )
                for u in range(2)
            ]
        )
        for hops in (0, 1, SIDE - 1, 2)
    ]


def on_device(
    activations, cotangents, left_root, right_root, block_owner, owned_sources, owner_counts
):
    owner_total = lax.axis_size("mp")
    layers, _, width = cotangents.shape
    slot_total, size = left_root.shape[2], left_root.shape[-1]
    cols = width // size
    blocks = layers * cols
    owners = block_owner.reshape(-1)
    group, holder = lax.axis_index("dp"), lax.axis_index("mp")
    chip_y, core = group // CORES, lax.rem(group, CORES)
    parity = lax.rem(holder, 2)

    for_chips = activations_for_chips(activations, chip_y, parity)
    from_chips = [for_chips[0]] + [
        along_y(piece, hops) for piece, hops in zip(for_chips[1:], (1, -1, 2))
    ]
    first, second = split_cotangents(owners, after(cotangents, *for_chips), owner_total)
    first = exchange(first)
    second = exchange(after(second, first))
    base = first.shape[1]

    halves = [jnp.stack([piece[u] for piece in from_chips]) for u in range(2)]
    first_parts = ring_in_two(first, along_y)
    pieces = (halves[0], halves[1], along_z(halves[0], 1), along_z(halves[1], -1))
    owner_of = second[:, base : base + blocks, 0].astype(jnp.int32)
    second = after(second[:, :base], *first_parts)
    second_parts = (second, along_y(second, 1), along_y(second, -1), along_y(second, 2))

    all_owners = jnp.arange(owner_total, dtype=jnp.int32)
    named = (owner_of[:, :, None] == all_owners).astype(jnp.int32)
    given = jnp.sum(named, axis=1)
    earlier = (all_owners[:, None] > all_owners[None, :]).astype(jnp.int32)
    slot_of = jnp.sum(earlier[:, :, None] * given[None, :, :], axis=1)
    slots = (owner_of * slot_total + jnp.sum(named * slot_of[:, None, :], axis=-1)).reshape(-1)

    def sliced_slots(here, parts):
        kept, given = gradient_partials(here, pieces, parts)
        return deal_to_slots(slots, kept, other_core(given), slot_total)

    slot_range = jnp.arange(slot_total, dtype=jnp.int32)
    sources = jnp.where(slot_range < owner_counts.reshape(()), owned_sources.reshape(-1), -1)
    here = jnp.stack((core, parity)).astype(jnp.int32)
    here, slots, sources = lax.optimization_barrier((here, slots, sources))
    dealt = sliced_slots(here, first_parts)
    arrived = exchange(dealt)
    dealt = sliced_slots(after(here, dealt), second_parts)
    dealt, arrived = lax.optimization_barrier((dealt, arrived))
    more = exchange(dealt)

    def by_slot(value):
        return value.reshape((owner_total, slot_total) + value.shape[1:])

    returning, left_stats, right_stats = work_on_slots(
        sources,
        left_root.reshape(slot_total, size, size),
        right_root.reshape(slot_total, size, size),
        (by_slot(arrived), by_slot(more)),
        owner_total,
    )
    precond = place_blocks(owners, exchange(returning), layers, cols)
    stat_shape = (1, 1, slot_total, size, size)
    return (precond, left_stats.reshape(stat_shape), right_stats.reshape(stat_shape))


def solution(mesh):
    placed = (
        P(None, "dp", None),
        P(None, "dp", "mp"),
        P("dp", "mp", None, None, None),
        P("dp", "mp", None, None, None),
        P("dp", "mp", None),
        P("dp", "mp", None),
        P("dp", "mp"),
    )
    return jax.shard_map(
        on_device,
        mesh=mesh,
        in_specs=placed,
        out_specs=(
            P(None, "dp", "mp"),
            P("dp", "mp", None, None, None),
            P("dp", "mp", None, None, None),
        ),
        check_vma=False,
    )
```

```python
import functools

import jax
import jax.numpy as jnp
from jax import lax
from jax.experimental import pallas as pl
from jax.experimental.pallas import tpu as pltpu
from jax.sharding import PartitionSpec as P

CHUNKS = 2
SIDE = 4
CORES = 2
TABLE_ROWS = 16
MIB = 1024 * 1024

NT = (((1,), (1,)), ((), ()))
NN = (((1,), (0,)), ((), ()))
TN = (((0,), (0,)), ((), ()))


def dot(a, b, dims):
    return lax.dot_general(a, b, dims, preferred_element_type=jnp.float32)


def along_y(value, hops):
    pairs = [
        (y * CORES + c, (y + hops) % SIDE * CORES + c) for y in range(SIDE) for c in range(CORES)
    ]
    return lax.ppermute(value, "dp", pairs)


def other_core(value):
    pairs = [(y * CORES + c, y * CORES + 1 - c) for y in range(SIDE) for c in range(CORES)]
    return lax.ppermute(value, "dp", pairs)


def along_z(value, hops):
    pairs = [(x * SIDE + z, x * SIDE + (z + hops) % SIDE) for x in range(SIDE) for z in range(SIDE)]
    return lax.ppermute(value, "mp", pairs)


def ring_in_two(value, move):
    half = value.shape[0] // 2
    before, behind = move(value, 1), move(value, -1)
    return (value, before, behind, move(before[:half], 1), move(behind[half:], -1))


def exchange(value):
    return lax.all_to_all(value, "mp", split_axis=0, concat_axis=0, tiled=True)


def after(value, *needed):
    return lax.optimization_barrier((value,) + needed)[0]


def split_kernel(owner_ref, cot_ref, *out_refs):
    layers, tokens, width = cot_ref.shape
    parts, piece = out_refs[0].shape[0], TABLE_ROWS
    size = parts * piece * CHUNKS
    cols = width // size
    for layer in range(layers):
        for col in range(cols):
            turned = cot_ref[layer, :, col * size : (col + 1) * size].T
            row = (layer * cols + col) * piece
            for q, out_ref in enumerate(out_refs):
                half = turned[q * parts * piece : (q + 1) * parts * piece]
                out_ref[:, row : row + piece, :] = half.reshape(parts, piece, tokens)
    rows = lax.broadcasted_iota(jnp.int32, (TABLE_ROWS, tokens), 0)
    table = jnp.zeros((TABLE_ROWS, tokens), jnp.float32)
    for t in range(layers * cols):
        table = jnp.where(rows == t, owner_ref[t].astype(jnp.float32), table)
    base, out_ref = layers * cols * piece, out_refs[-1]
    for part in range(parts):
        out_ref[part, base : base + TABLE_ROWS, :] = table.astype(out_ref.dtype)


def split_cotangents(owners, cotangents, owner_total):
    layers, tokens, width = cotangents.shape
    rows = width * layers // owner_total // CHUNKS
    return pl.pallas_call(
        split_kernel,
        in_specs=[
            pl.BlockSpec(memory_space=pltpu.SMEM),
            pl.BlockSpec(memory_space=pltpu.VMEM),
        ],
        out_specs=[pl.BlockSpec(memory_space=pltpu.VMEM)] * 2,
        out_shape=[
            jax.ShapeDtypeStruct((owner_total, rows, tokens), cotangents.dtype),
            jax.ShapeDtypeStruct((owner_total, rows + TABLE_ROWS, tokens), cotangents.dtype),
        ],
        compiler_params=pltpu.CompilerParams(vmem_limit_bytes=6 * MIB),
        cost_estimate=pl.CostEstimate(
            flops=0, bytes_accessed=4 * cotangents.size, transcendentals=0
        ),
        name="split_cotangents",
    )(owners, cotangents)


def partial_kernel(here_ref, *refs):
    pieces, parts, (kept_ref, given_ref, acts, held, sems) = refs[:4], refs[4:-5], refs[-5:]
    _, layers, count, _ = pieces[0].shape
    _, holders, all_rows, tokens = held.shape
    width = kept_ref.shape[-1]
    rows, half = all_rows // layers, holders // 2

    def fetches(layer):
        moves = []
        for n, part in enumerate(parts):
            to = held.at[min(n, 3)]
            if part.shape[0] == half:
                to = to.at[pl.ds((n - 3) * half, half)]
            mine = pl.ds(layer * rows, rows)
            moves.append((part.at[:, mine, :], to.at[:, mine, :]))
        for n, piece in enumerate(pieces):
            first = here_ref[1] if n < 2 else 1 - here_ref[1]
            start = pl.multiple_of((first * 2 + n % 2) * count, count)
            moves.append((piece.at[:, layer], acts.at[layer, :, pl.ds(start, count), :]))
        return [pltpu.make_async_copy(*move, sems.at[layer, n]) for n, move in enumerate(moves)]

    for layer in range(layers):
        for fetch in fetches(layer):
            fetch.start()
    for layer in range(layers):
        for fetch in fetches(layer):
            fetch.wait()
        mine = slice(layer * rows, (layer + 1) * rows)
        for side in range(2):
            some = slice(side * half, (side + 1) * half)
            flat = [held[n, some, mine, :].reshape(half * rows, tokens) for n in range(4)]
            for out_ref, which in ((kept_ref, here_ref[0]), (given_ref, 1 - here_ref[0])):
                columns = pl.ds(pl.multiple_of(which * width, width), width)
                total = dot(flat[0], acts[layer, 0, :, columns], NN)
                for n in range(1, SIDE):
                    total += dot(flat[n], acts[layer, n, :, columns], NN)
                out_ref[some, mine, :] = total.astype(out_ref.dtype).reshape(half, rows, width)


def gradient_partials(here, pieces, parts):
    chips, layers, _, width = pieces[0].shape
    holders, all_rows, tokens = parts[0].shape
    kind = parts[0].dtype
    shape = jax.ShapeDtypeStruct((holders, all_rows, width // CORES), kind)
    inputs = len(pieces) + len(parts)
    return pl.pallas_call(
        partial_kernel,
        in_specs=[pl.BlockSpec(memory_space=pltpu.SMEM)]
        + [pl.BlockSpec(memory_space=pl.ANY)] * inputs,
        out_specs=[pl.BlockSpec(memory_space=pltpu.VMEM)] * 2,
        scratch_shapes=[
            pltpu.VMEM((layers, chips, tokens, width), kind),
            pltpu.VMEM((SIDE, holders, all_rows, tokens), kind),
            pltpu.SemaphoreType.DMA((layers, inputs)),
        ],
        out_shape=[shape, shape],
        compiler_params=pltpu.CompilerParams(vmem_limit_bytes=50 * MIB),
        cost_estimate=pl.CostEstimate(flops=0, bytes_accessed=1024, transcendentals=0),
        name="gradient_partials",
    )(here, *pieces, *parts)


def deal_kernel(slot_ref, kept_ref, got_ref, out_ref):
    layer, half = pl.program_id(0), pl.program_id(1)
    holders, rows, _ = kept_ref.shape
    piece = out_ref.shape[1]
    cols = rows // piece
    for holder in range(holders):
        total = kept_ref[holder].astype(jnp.float32) + got_ref[holder].astype(jnp.float32)
        total = total.astype(out_ref.dtype)
        for col in range(cols):
            slot = slot_ref[((half * holders + holder) * 2 + layer) * cols + col]
            out_ref[slot] = total[col * piece : (col + 1) * piece]


def deal_to_slots(slots, kept, got, slot_total):
    holders, all_rows, size = kept.shape
    layers = 2
    rows = all_rows // layers
    shape = (holders * slot_total, TABLE_ROWS, size)
    return pl.pallas_call(
        deal_kernel,
        grid_spec=pltpu.PrefetchScalarGridSpec(
            num_scalar_prefetch=1,
            grid=(layers, 2),
            in_specs=[pl.BlockSpec((holders // 2, rows, size), lambda l, h, s: (h, l, 0))] * 2,
            out_specs=pl.BlockSpec(shape, lambda l, h, s: (0, 0, 0)),
        ),
        out_shape=jax.ShapeDtypeStruct(shape, kept.dtype),
        compiler_params=pltpu.CompilerParams(vmem_limit_bytes=6 * MIB),
        cost_estimate=pl.CostEstimate(flops=0, bytes_accessed=1024, transcendentals=0),
        name="deal_to_slots",
    )(slots, kept, got)


def slot_kernel(source_ref, left_ref, right_ref, first_ref, second_ref, *refs):
    out_ref, left_stat_ref, right_stat_ref, lefts, rights, turns, sems = refs
    slot = pl.program_id(0)
    slot_total, size, _ = lefts.shape

    def fetches(s):
        moves = [(left_ref.at[s], lefts.at[s]), (right_ref.at[s], rights.at[s])]
        moves += [(ref.at[:, s], turns.at[s, q]) for q, ref in enumerate((first_ref, second_ref))]
        return [pltpu.make_async_copy(*move, sems.at[s, n]) for n, move in enumerate(moves)]

    @pl.when(slot == 0)
    def _():
        for s in range(slot_total):
            for fetch in fetches(s):
                fetch.start()

    for fetch in fetches(slot):
        fetch.wait()
    is_live = source_ref[slot] >= 0

    @pl.when(is_live)
    def _():
        turned = turns[slot].reshape(size, size)
        inner = dot(lefts[slot], turned, NT).astype(out_ref.dtype)
        out_ref[0] = dot(inner, rights[slot], NN).astype(out_ref.dtype)
        scale = 1.0 / size
        left_stat_ref[0] = (dot(turned, turned, TN) * scale).astype(left_stat_ref.dtype)
        right_stat_ref[0] = (dot(turned, turned, NT) * scale).astype(right_stat_ref.dtype)

    @pl.when(jnp.logical_not(is_live))
    def _():
        left_stat_ref[...] = jnp.zeros_like(left_stat_ref)
        right_stat_ref[...] = jnp.zeros_like(right_stat_ref)


def work_on_slots(sources, left_roots, right_roots, arrived, owner_total):
    slot_total, size, _ = left_roots.shape
    kind = left_roots.dtype
    slices = arrived[0].shape

    def out_place(s, source):
        place = source[s]
        for back in range(1, slot_total):
            place = jnp.where(place >= 0, place, source[jnp.maximum(s - back, 0)])
        return (place, 0, 0)

    def live(s, source):
        return (s, 0, 0)

    stats = jax.ShapeDtypeStruct((slot_total, size, size), kind)
    return pl.pallas_call(
        slot_kernel,
        grid_spec=pltpu.PrefetchScalarGridSpec(
            num_scalar_prefetch=1,
            grid=(slot_total,),
            in_specs=[pl.BlockSpec(memory_space=pl.ANY)] * 4,
            out_specs=[
                pl.BlockSpec((1, size, size), out_place),
                pl.BlockSpec((1, size, size), live),
                pl.BlockSpec((1, size, size), live),
            ],
            scratch_shapes=[
                pltpu.VMEM((slot_total, size, size), kind),
                pltpu.VMEM((slot_total, size, size), kind),
                pltpu.VMEM((slot_total, CHUNKS, slices[0], slices[2], size), kind),
                pltpu.SemaphoreType.DMA((slot_total, 4)),
            ],
        ),
        out_shape=[jax.ShapeDtypeStruct((owner_total, size, size), kind), stats, stats],
        compiler_params=pltpu.CompilerParams(vmem_limit_bytes=50 * MIB),
        cost_estimate=pl.CostEstimate(
            flops=8 * slot_total * size**3,
            bytes_accessed=12 * slot_total * size * size,
            transcendentals=0,
        ),
        name="work_on_slots",
    )(sources, left_roots, right_roots, *arrived)


def place_kernel(owner_ref, returned_ref, out_ref, held, in_sems, out_sems):
    layers, size, width = out_ref.shape
    cols = width // size
    blocks = [(l, c, l * cols + c) for l in range(layers) for c in range(cols)]
    fetches = [
        pltpu.make_async_copy(returned_ref.at[owner_ref[t]], held.at[t], in_sems.at[t])
        for _, _, t in blocks
    ]
    stores = [
        pltpu.make_async_copy(
            held.at[t], out_ref.at[l, :, pl.ds(c * size, size)], out_sems.at[t]
        )
        for l, c, t in blocks
    ]
    for fetch in fetches:
        fetch.start()
    for fetch, store in zip(fetches, stores):
        fetch.wait()
        store.start()
    for store in stores:
        store.wait()


def place_blocks(owners, returned, layers, cols):
    _, size, _ = returned.shape
    return pl.pallas_call(
        place_kernel,
        in_specs=[
            pl.BlockSpec(memory_space=pltpu.SMEM),
            pl.BlockSpec(memory_space=pl.ANY),
        ],
        out_specs=pl.BlockSpec(memory_space=pl.ANY),
        out_shape=jax.ShapeDtypeStruct((layers, size, cols * size), returned.dtype),
        scratch_shapes=[
            pltpu.VMEM((layers * cols, size, size), returned.dtype),
            pltpu.SemaphoreType.DMA((layers * cols,)),
            pltpu.SemaphoreType.DMA((layers * cols,)),
        ],
        compiler_params=pltpu.CompilerParams(vmem_limit_bytes=8 * MIB),
        cost_estimate=pl.CostEstimate(
            flops=0, bytes_accessed=4 * layers * cols * size * size, transcendentals=0
        ),
        name="place_blocks",
    )(owners, returned)


def activations_for_chips(activations, chip_y, parity):
    layers, tokens, width = activations.shape
    rows, pair_width = tokens // 4, width // SIDE
    return [
        jnp.stack(
            [
                lax.dynamic_slice(
                    activations,
                    (0, (parity * 2 + u) * rows, lax.rem(chip_y + hops, SIDE) * pair_width),
                    (layers, rows, pair_width),
                )
                for u in range(2)
            ]
        )
        for hops in (0, 1, SIDE - 1, 2)
    ]


def on_device(
    activations, cotangents, left_root, right_root, block_owner, owned_sources, owner_counts
):
    owner_total = lax.axis_size("mp")
    layers, _, width = cotangents.shape
    slot_total, size = left_root.shape[2], left_root.shape[-1]
    cols = width // size
    blocks = layers * cols
    owners = block_owner.reshape(-1)
    group, holder = lax.axis_index("dp"), lax.axis_index("mp")
    chip_y, core = group // CORES, lax.rem(group, CORES)
    parity = lax.rem(holder, 2)

    for_chips = activations_for_chips(activations, chip_y, parity)
    from_chips = [for_chips[0]] + [
        along_y(piece, hops) for piece, hops in zip(for_chips[1:], (1, -1, 2))
    ]
    first, second = split_cotangents(owners, after(cotangents, *for_chips), owner_total)
    first = exchange(first)
    second = exchange(after(second, first))
    base = first.shape[1]

    halves = [jnp.stack([piece[u] for piece in from_chips]) for u in range(2)]
    first_parts = ring_in_two(first, along_y)
    pieces = (halves[0], halves[1], along_z(halves[0], 1), along_z(halves[1], -1))
    owner_of = second[:, base : base + blocks, 0].astype(jnp.int32)

    all_owners = jnp.arange(owner_total, dtype=jnp.int32)
    named = (owner_of[:, :, None] == all_owners).astype(jnp.int32)
    given = jnp.sum(named, axis=1)
    earlier = (all_owners[:, None] > all_owners[None, :]).astype(jnp.int32)
    slot_of = jnp.sum(earlier[:, :, None] * given[None, :, :], axis=1)
    slots = (owner_of * slot_total + jnp.sum(named * slot_of[:, None, :], axis=-1)).reshape(-1)

    def sliced_slots(here, parts):
        kept, given = gradient_partials(here, pieces, parts)
        return deal_to_slots(slots, kept, other_core(given), slot_total)

    slot_range = jnp.arange(slot_total, dtype=jnp.int32)
    sources = jnp.where(slot_range < owner_counts.reshape(()), owned_sources.reshape(-1), -1)
    here = jnp.stack((core, parity)).astype(jnp.int32)
    here, slots, sources, second = lax.optimization_barrier(
        (here, slots, sources, second[:, :base], first_parts[1:3])
    )[:4]
    second_parts = (second, along_y(second, 1), along_y(second, -1), along_y(second, 2))
    dealt = sliced_slots(here, first_parts)
    arrived = exchange(dealt)
    dealt = sliced_slots(after(here, dealt), second_parts)
    dealt, arrived = lax.optimization_barrier((dealt, arrived))
    more = exchange(dealt)

    def by_slot(value):
        return value.reshape((owner_total, slot_total) + value.shape[1:])

    returning, left_stats, right_stats = work_on_slots(
        sources,
        left_root.reshape(slot_total, size, size),
        right_root.reshape(slot_total, size, size),
        (by_slot(arrived), by_slot(more)),
        owner_total,
    )
    precond = place_blocks(owners, exchange(returning), layers, cols)
    stat_shape = (1, 1, slot_total, size, size)
    return (precond, left_stats.reshape(stat_shape), right_stats.reshape(stat_shape))


def solution(mesh):
    placed = (
        P(None, "dp", None),
        P(None, "dp", "mp"),
        P("dp", "mp", None, None, None),
        P("dp", "mp", None, None, None),
        P("dp", "mp", None),
        P("dp", "mp", None),
        P("dp", "mp"),
    )
    return jax.shard_map(
        on_device,
        mesh=mesh,
        in_specs=placed,
        out_specs=(
            P(None, "dp", "mp"),
            P("dp", "mp", None, None, None),
            P("dp", "mp", None, None, None),
        ),
        check_vma=False,
    )
```

```python
import functools

import jax
import jax.numpy as jnp
from jax import lax
from jax.experimental import pallas as pl
from jax.experimental.pallas import tpu as pltpu
from jax.sharding import PartitionSpec as P

CHUNKS = 2
SIDE = 4
CORES = 2
TABLE_ROWS = 16
MIB = 1024 * 1024

NT = (((1,), (1,)), ((), ()))
NN = (((1,), (0,)), ((), ()))
TN = (((0,), (0,)), ((), ()))


def dot(a, b, dims):
    return lax.dot_general(a, b, dims, preferred_element_type=jnp.float32)


def along_y(value, hops):
    pairs = [
        (y * CORES + c, (y + hops) % SIDE * CORES + c) for y in range(SIDE) for c in range(CORES)
    ]
    return lax.ppermute(value, "dp", pairs)


def other_core(value):
    pairs = [(y * CORES + c, y * CORES + 1 - c) for y in range(SIDE) for c in range(CORES)]
    return lax.ppermute(value, "dp", pairs)


def along_z(value, hops):
    pairs = [(x * SIDE + z, x * SIDE + (z + hops) % SIDE) for x in range(SIDE) for z in range(SIDE)]
    return lax.ppermute(value, "mp", pairs)


def ring_in_two(value, move):
    half = value.shape[0] // 2
    before, behind = move(value, 1), move(value, -1)
    return (value, before, behind, move(before[:half], 1), move(behind[half:], -1))


def exchange(value):
    return lax.all_to_all(value, "mp", split_axis=0, concat_axis=0, tiled=True)


def after(value, *needed):
    return lax.optimization_barrier((value,) + needed)[0]


def split_kernel(owner_ref, cot_ref, *out_refs):
    layers, tokens, width = cot_ref.shape
    parts, piece = out_refs[0].shape[0], TABLE_ROWS
    size = parts * piece * CHUNKS
    cols = width // size
    for layer in range(layers):
        for col in range(cols):
            turned = cot_ref[layer, :, col * size : (col + 1) * size].T
            row = (layer * cols + col) * piece
            for q, out_ref in enumerate(out_refs):
                half = turned[q * parts * piece : (q + 1) * parts * piece]
                out_ref[:, row : row + piece, :] = half.reshape(parts, piece, tokens)
    rows = lax.broadcasted_iota(jnp.int32, (TABLE_ROWS, tokens), 0)
    table = jnp.zeros((TABLE_ROWS, tokens), jnp.float32)
    for t in range(layers * cols):
        table = jnp.where(rows == t, owner_ref[t].astype(jnp.float32), table)
    base, out_ref = layers * cols * piece, out_refs[-1]
    for part in range(parts):
        out_ref[part, base : base + TABLE_ROWS, :] = table.astype(out_ref.dtype)


def split_cotangents(owners, cotangents, owner_total):
    layers, tokens, width = cotangents.shape
    rows = width * layers // owner_total // CHUNKS
    return pl.pallas_call(
        split_kernel,
        in_specs=[
            pl.BlockSpec(memory_space=pltpu.SMEM),
            pl.BlockSpec(memory_space=pltpu.VMEM),
        ],
        out_specs=[pl.BlockSpec(memory_space=pltpu.VMEM)] * 2,
        out_shape=[
            jax.ShapeDtypeStruct((owner_total, rows, tokens), cotangents.dtype),
            jax.ShapeDtypeStruct((owner_total, rows + TABLE_ROWS, tokens), cotangents.dtype),
        ],
        compiler_params=pltpu.CompilerParams(vmem_limit_bytes=6 * MIB),
        cost_estimate=pl.CostEstimate(
            flops=0, bytes_accessed=4 * cotangents.size, transcendentals=0
        ),
        name="split_cotangents",
    )(owners, cotangents)


def partial_kernel(here_ref, *refs):
    pieces, parts, (kept_ref, given_ref, acts, held, sems) = refs[:4], refs[4:-5], refs[-5:]
    _, layers, count, _ = pieces[0].shape
    _, holders, all_rows, tokens = held.shape
    width = kept_ref.shape[-1]
    rows, half = all_rows // layers, holders // 2

    def fetches(layer):
        moves = []
        for n, part in enumerate(parts):
            to = held.at[min(n, 3)]
            if part.shape[0] == half:
                to = to.at[pl.ds((n - 3) * half, half)]
            mine = pl.ds(layer * rows, rows)
            moves.append((part.at[:, mine, :], to.at[:, mine, :]))
        for n, piece in enumerate(pieces):
            first = here_ref[1] if n < 2 else 1 - here_ref[1]
            start = pl.multiple_of((first * 2 + n % 2) * count, count)
            moves.append((piece.at[:, layer], acts.at[layer, :, pl.ds(start, count), :]))
        return [pltpu.make_async_copy(*move, sems.at[layer, n]) for n, move in enumerate(moves)]

    for layer in range(layers):
        for fetch in fetches(layer):
            fetch.start()
    for layer in range(layers):
        for fetch in fetches(layer):
            fetch.wait()
        mine = slice(layer * rows, (layer + 1) * rows)
        for side in range(2):
            some = slice(side * half, (side + 1) * half)
            flat = [held[n, some, mine, :].reshape(half * rows, tokens) for n in range(4)]
            for out_ref, which in ((kept_ref, here_ref[0]), (given_ref, 1 - here_ref[0])):
                columns = pl.ds(pl.multiple_of(which * width, width), width)
                total = dot(flat[0], acts[layer, 0, :, columns], NN)
                for n in range(1, SIDE):
                    total += dot(flat[n], acts[layer, n, :, columns], NN)
                out_ref[some, mine, :] = total.astype(out_ref.dtype).reshape(half, rows, width)


def gradient_partials(here, pieces, parts):
    chips, layers, _, width = pieces[0].shape
    holders, all_rows, tokens = parts[0].shape
    kind = parts[0].dtype
    shape = jax.ShapeDtypeStruct((holders, all_rows, width // CORES), kind)
    inputs = len(pieces) + len(parts)
    return pl.pallas_call(
        partial_kernel,
        in_specs=[pl.BlockSpec(memory_space=pltpu.SMEM)]
        + [pl.BlockSpec(memory_space=pl.ANY)] * inputs,
        out_specs=[pl.BlockSpec(memory_space=pltpu.VMEM)] * 2,
        scratch_shapes=[
            pltpu.VMEM((layers, chips, tokens, width), kind),
            pltpu.VMEM((SIDE, holders, all_rows, tokens), kind),
            pltpu.SemaphoreType.DMA((layers, inputs)),
        ],
        out_shape=[shape, shape],
        compiler_params=pltpu.CompilerParams(vmem_limit_bytes=36 * MIB),
        cost_estimate=pl.CostEstimate(flops=0, bytes_accessed=1024, transcendentals=0),
        name="gradient_partials",
    )(here, *pieces, *parts)


def deal_kernel(slot_ref, kept_ref, got_ref, out_ref):
    layer, half = pl.program_id(0), pl.program_id(1)
    holders, rows, _ = kept_ref.shape
    piece = out_ref.shape[1]
    cols = rows // piece
    for holder in range(holders):
        total = kept_ref[holder].astype(jnp.float32) + got_ref[holder].astype(jnp.float32)
        total = total.astype(out_ref.dtype)
        for col in range(cols):
            slot = slot_ref[((half * holders + holder) * 2 + layer) * cols + col]
            out_ref[slot] = total[col * piece : (col + 1) * piece]


def deal_to_slots(slots, kept, got, slot_total):
    holders, all_rows, size = kept.shape
    layers = 2
    rows = all_rows // layers
    shape = (holders * slot_total, TABLE_ROWS, size)
    return pl.pallas_call(
        deal_kernel,
        grid_spec=pltpu.PrefetchScalarGridSpec(
            num_scalar_prefetch=1,
            grid=(layers, 2),
            in_specs=[pl.BlockSpec((holders // 2, rows, size), lambda l, h, s: (h, l, 0))] * 2,
            out_specs=pl.BlockSpec(shape, lambda l, h, s: (0, 0, 0)),
        ),
        out_shape=jax.ShapeDtypeStruct(shape, kept.dtype),
        compiler_params=pltpu.CompilerParams(vmem_limit_bytes=6 * MIB),
        cost_estimate=pl.CostEstimate(flops=0, bytes_accessed=1024, transcendentals=0),
        name="deal_to_slots",
    )(slots, kept, got)


def slot_kernel(source_ref, left_ref, right_ref, first_ref, second_ref, *refs):
    out_ref, left_stat_ref, right_stat_ref, lefts, rights, turns, sems = refs
    slot = pl.program_id(0)
    slot_total, size, _ = lefts.shape

    def fetches(s):
        moves = [(left_ref.at[s], lefts.at[s]), (right_ref.at[s], rights.at[s])]
        moves += [(ref.at[:, s], turns.at[s, q]) for q, ref in enumerate((first_ref, second_ref))]
        return [pltpu.make_async_copy(*move, sems.at[s, n]) for n, move in enumerate(moves)]

    @pl.when(slot == 0)
    def _():
        for s in range(slot_total):
            for fetch in fetches(s):
                fetch.start()

    for fetch in fetches(slot):
        fetch.wait()
    is_live = source_ref[slot] >= 0

    @pl.when(is_live)
    def _():
        turned = turns[slot].reshape(size, size)
        inner = dot(lefts[slot], turned, NT).astype(out_ref.dtype)
        out_ref[0] = dot(inner, rights[slot], NN).astype(out_ref.dtype)
        scale = 1.0 / size
        left_stat_ref[0] = (dot(turned, turned, TN) * scale).astype(left_stat_ref.dtype)
        right_stat_ref[0] = (dot(turned, turned, NT) * scale).astype(right_stat_ref.dtype)

    @pl.when(jnp.logical_not(is_live))
    def _():
        left_stat_ref[...] = jnp.zeros_like(left_stat_ref)
        right_stat_ref[...] = jnp.zeros_like(right_stat_ref)


def work_on_slots(sources, left_roots, right_roots, arrived, owner_total):
    slot_total, size, _ = left_roots.shape
    kind = left_roots.dtype
    slices = arrived[0].shape

    def out_place(s, source):
        place = source[s]
        for back in range(1, slot_total):
            place = jnp.where(place >= 0, place, source[jnp.maximum(s - back, 0)])
        return (place, 0, 0)

    def live(s, source):
        return (s, 0, 0)

    stats = jax.ShapeDtypeStruct((slot_total, size, size), kind)
    return pl.pallas_call(
        slot_kernel,
        grid_spec=pltpu.PrefetchScalarGridSpec(
            num_scalar_prefetch=1,
            grid=(slot_total,),
            in_specs=[pl.BlockSpec(memory_space=pl.ANY)] * 4,
            out_specs=[
                pl.BlockSpec((1, size, size), out_place),
                pl.BlockSpec((1, size, size), live),
                pl.BlockSpec((1, size, size), live),
            ],
            scratch_shapes=[
                pltpu.VMEM((slot_total, size, size), kind),
                pltpu.VMEM((slot_total, size, size), kind),
                pltpu.VMEM((slot_total, CHUNKS, slices[0], slices[2], size), kind),
                pltpu.SemaphoreType.DMA((slot_total, 4)),
            ],
        ),
        out_shape=[jax.ShapeDtypeStruct((owner_total, size, size), kind), stats, stats],
        compiler_params=pltpu.CompilerParams(vmem_limit_bytes=50 * MIB),
        cost_estimate=pl.CostEstimate(
            flops=8 * slot_total * size**3,
            bytes_accessed=12 * slot_total * size * size,
            transcendentals=0,
        ),
        name="work_on_slots",
    )(sources, left_roots, right_roots, *arrived)


def place_kernel(owner_ref, returned_ref, out_ref, held, in_sems, out_sems):
    layers, size, width = out_ref.shape
    cols = width // size
    blocks = [(l, c, l * cols + c) for l in range(layers) for c in range(cols)]
    fetches = [
        pltpu.make_async_copy(returned_ref.at[owner_ref[t]], held.at[t], in_sems.at[t])
        for _, _, t in blocks
    ]
    stores = [
        pltpu.make_async_copy(
            held.at[t], out_ref.at[l, :, pl.ds(c * size, size)], out_sems.at[t]
        )
        for l, c, t in blocks
    ]
    for fetch in fetches:
        fetch.start()
    for fetch, store in zip(fetches, stores):
        fetch.wait()
        store.start()
    for store in stores:
        store.wait()


def place_blocks(owners, returned, layers, cols):
    _, size, _ = returned.shape
    return pl.pallas_call(
        place_kernel,
        in_specs=[
            pl.BlockSpec(memory_space=pltpu.SMEM),
            pl.BlockSpec(memory_space=pl.ANY),
        ],
        out_specs=pl.BlockSpec(memory_space=pl.ANY),
        out_shape=jax.ShapeDtypeStruct((layers, size, cols * size), returned.dtype),
        scratch_shapes=[
            pltpu.VMEM((layers * cols, size, size), returned.dtype),
            pltpu.SemaphoreType.DMA((layers * cols,)),
            pltpu.SemaphoreType.DMA((layers * cols,)),
        ],
        compiler_params=pltpu.CompilerParams(vmem_limit_bytes=8 * MIB),
        cost_estimate=pl.CostEstimate(
            flops=0, bytes_accessed=4 * layers * cols * size * size, transcendentals=0
        ),
        name="place_blocks",
    )(owners, returned)


def activations_for_chips(activations, chip_y, parity):
    layers, tokens, width = activations.shape
    rows, pair_width = tokens // 4, width // SIDE
    return [
        jnp.stack(
            [
                lax.dynamic_slice(
                    activations,
                    (0, (parity * 2 + u) * rows, lax.rem(chip_y + hops, SIDE) * pair_width),
                    (layers, rows, pair_width),
                )
                for u in range(2)
            ]
        )
        for hops in (0, 1, SIDE - 1, 2)
    ]


def on_device(
    activations, cotangents, left_root, right_root, block_owner, owned_sources, owner_counts
):
    owner_total = lax.axis_size("mp")
    layers, _, width = cotangents.shape
    slot_total, size = left_root.shape[2], left_root.shape[-1]
    cols = width // size
    blocks = layers * cols
    owners = block_owner.reshape(-1)
    group, holder = lax.axis_index("dp"), lax.axis_index("mp")
    chip_y, core = group // CORES, lax.rem(group, CORES)
    parity = lax.rem(holder, 2)

    for_chips = activations_for_chips(activations, chip_y, parity)
    from_chips = [for_chips[0]] + [
        along_y(piece, hops) for piece, hops in zip(for_chips[1:], (1, -1, 2))
    ]
    first, second = split_cotangents(owners, after(cotangents, *for_chips), owner_total)
    first = exchange(first)
    second = exchange(after(second, first))
    base = first.shape[1]

    halves = [jnp.stack([piece[u] for piece in from_chips]) for u in range(2)]
    first_parts = ring_in_two(first, along_y)
    pieces = (halves[0], halves[1], along_z(halves[0], 1), along_z(halves[1], -1))
    owner_of = second[:, base : base + blocks, 0].astype(jnp.int32)

    all_owners = jnp.arange(owner_total, dtype=jnp.int32)
    named = (owner_of[:, :, None] == all_owners).astype(jnp.int32)
    given = jnp.sum(named, axis=1)
    earlier = (all_owners[:, None] > all_owners[None, :]).astype(jnp.int32)
    slot_of = jnp.sum(earlier[:, :, None] * given[None, :, :], axis=1)
    slots = (owner_of * slot_total + jnp.sum(named * slot_of[:, None, :], axis=-1)).reshape(-1)

    def sliced_slots(here, parts):
        kept, given = gradient_partials(here, pieces, parts)
        return deal_to_slots(slots, kept, other_core(given), slot_total)

    slot_range = jnp.arange(slot_total, dtype=jnp.int32)
    sources = jnp.where(slot_range < owner_counts.reshape(()), owned_sources.reshape(-1), -1)
    here = jnp.stack((core, parity)).astype(jnp.int32)
    here, slots, sources, second = lax.optimization_barrier(
        (here, slots, sources, second[:, :base], first_parts[1:3])
    )[:4]
    second_parts = (second, along_y(second, 1), along_y(second, -1), along_y(second, 2))
    dealt = sliced_slots(here, first_parts)
    arrived = exchange(dealt)
    dealt = sliced_slots(after(here, dealt), second_parts)
    dealt, arrived = lax.optimization_barrier((dealt, arrived))
    more = exchange(dealt)

    def by_slot(value):
        return value.reshape((owner_total, slot_total) + value.shape[1:])

    returning, left_stats, right_stats = work_on_slots(
        sources,
        left_root.reshape(slot_total, size, size),
        right_root.reshape(slot_total, size, size),
        (by_slot(arrived), by_slot(more)),
        owner_total,
    )
    precond = place_blocks(owners, exchange(returning), layers, cols)
    stat_shape = (1, 1, slot_total, size, size)
    return (precond, left_stats.reshape(stat_shape), right_stats.reshape(stat_shape))


def solution(mesh):
    placed = (
        P(None, "dp", None),
        P(None, "dp", "mp"),
        P("dp", "mp", None, None, None),
        P("dp", "mp", None, None, None),
        P("dp", "mp", None),
        P("dp", "mp", None),
        P("dp", "mp"),
    )
    return jax.shard_map(
        on_device,
        mesh=mesh,
        in_specs=placed,
        out_specs=(
            P(None, "dp", "mp"),
            P("dp", "mp", None, None, None),
            P("dp", "mp", None, None, None),
        ),
        check_vma=False,
    )
```

```python
import functools

import jax
import jax.numpy as jnp
from jax import lax
from jax.experimental import pallas as pl
from jax.experimental.pallas import tpu as pltpu
from jax.sharding import PartitionSpec as P

CHUNKS = 2
SIDE = 4
CORES = 2
TABLE_ROWS = 16
MIB = 1024 * 1024

NT = (((1,), (1,)), ((), ()))
NN = (((1,), (0,)), ((), ()))
TN = (((0,), (0,)), ((), ()))


def dot(a, b, dims):
    return lax.dot_general(a, b, dims, preferred_element_type=jnp.float32)


def along_y(value, hops):
    pairs = [
        (y * CORES + c, (y + hops) % SIDE * CORES + c) for y in range(SIDE) for c in range(CORES)
    ]
    return lax.ppermute(value, "dp", pairs)


def other_core(value):
    pairs = [(y * CORES + c, y * CORES + 1 - c) for y in range(SIDE) for c in range(CORES)]
    return lax.ppermute(value, "dp", pairs)


def along_z(value, hops):
    pairs = [(x * SIDE + z, x * SIDE + (z + hops) % SIDE) for x in range(SIDE) for z in range(SIDE)]
    return lax.ppermute(value, "mp", pairs)


def ring_in_two(value, move):
    half = value.shape[0] // 2
    before, behind = move(value, 1), move(value, -1)
    return (value, before, behind, move(before[:half], 1), move(behind[half:], -1))


def exchange(value):
    return lax.all_to_all(value, "mp", split_axis=0, concat_axis=0, tiled=True)


def after(value, *needed):
    return lax.optimization_barrier((value,) + needed)[0]


def split_kernel(owner_ref, cot_ref, *out_refs):
    layers, tokens, width = cot_ref.shape
    parts, piece = out_refs[0].shape[0], TABLE_ROWS
    size = parts * piece * CHUNKS
    cols = width // size
    for layer in range(layers):
        for col in range(cols):
            turned = cot_ref[layer, :, col * size : (col + 1) * size].T
            row = (layer * cols + col) * piece
            for q, out_ref in enumerate(out_refs):
                half = turned[q * parts * piece : (q + 1) * parts * piece]
                out_ref[:, row : row + piece, :] = half.reshape(parts, piece, tokens)
    rows = lax.broadcasted_iota(jnp.int32, (TABLE_ROWS, tokens), 0)
    table = jnp.zeros((TABLE_ROWS, tokens), jnp.float32)
    for t in range(layers * cols):
        table = jnp.where(rows == t, owner_ref[t].astype(jnp.float32), table)
    base, out_ref = layers * cols * piece, out_refs[-1]
    for part in range(parts):
        out_ref[part, base : base + TABLE_ROWS, :] = table.astype(out_ref.dtype)


def split_cotangents(owners, cotangents, owner_total):
    layers, tokens, width = cotangents.shape
    rows = width * layers // owner_total // CHUNKS
    return pl.pallas_call(
        split_kernel,
        in_specs=[
            pl.BlockSpec(memory_space=pltpu.SMEM),
            pl.BlockSpec(memory_space=pltpu.VMEM),
        ],
        out_specs=[pl.BlockSpec(memory_space=pltpu.VMEM)] * 2,
        out_shape=[
            jax.ShapeDtypeStruct((owner_total, rows, tokens), cotangents.dtype),
            jax.ShapeDtypeStruct((owner_total, rows + TABLE_ROWS, tokens), cotangents.dtype),
        ],
        compiler_params=pltpu.CompilerParams(vmem_limit_bytes=6 * MIB),
        cost_estimate=pl.CostEstimate(
            flops=0, bytes_accessed=4 * cotangents.size, transcendentals=0
        ),
        name="split_cotangents",
    )(owners, cotangents)


def partial_kernel(here_ref, *refs):
    pieces, parts, (kept_ref, given_ref, acts, held, sems) = refs[:4], refs[4:-5], refs[-5:]
    _, layers, count, _ = pieces[0].shape
    _, holders, all_rows, tokens = held.shape
    width = kept_ref.shape[-1]
    rows, half = all_rows // layers, holders // 2

    def fetches(layer):
        moves = []
        for n, part in enumerate(parts):
            to = held.at[min(n, 3)]
            if part.shape[0] == half:
                to = to.at[pl.ds((n - 3) * half, half)]
            mine = pl.ds(layer * rows, rows)
            moves.append((part.at[:, mine, :], to.at[:, mine, :]))
        for n, piece in enumerate(pieces):
            first = here_ref[1] if n < 2 else 1 - here_ref[1]
            start = pl.multiple_of((first * 2 + n % 2) * count, count)
            moves.append((piece.at[:, layer], acts.at[layer, :, pl.ds(start, count), :]))
        return [pltpu.make_async_copy(*move, sems.at[layer, n]) for n, move in enumerate(moves)]

    for layer in range(layers):
        for fetch in fetches(layer):
            fetch.start()
    for layer in range(layers):
        for fetch in fetches(layer):
            fetch.wait()
        mine = slice(layer * rows, (layer + 1) * rows)
        for side in range(2):
            some = slice(side * half, (side + 1) * half)
            flat = [held[n, some, mine, :].reshape(half * rows, tokens) for n in range(4)]
            for out_ref, which in ((kept_ref, here_ref[0]), (given_ref, 1 - here_ref[0])):
                columns = pl.ds(pl.multiple_of(which * width, width), width)
                total = dot(flat[0], acts[layer, 0, :, columns], NN)
                for n in range(1, SIDE):
                    total += dot(flat[n], acts[layer, n, :, columns], NN)
                out_ref[some, mine, :] = total.astype(out_ref.dtype).reshape(half, rows, width)


def gradient_partials(here, pieces, parts):
    chips, layers, _, width = pieces[0].shape
    holders, all_rows, tokens = parts[0].shape
    kind = parts[0].dtype
    shape = jax.ShapeDtypeStruct((holders, all_rows, width // CORES), kind)
    inputs = len(pieces) + len(parts)
    return pl.pallas_call(
        partial_kernel,
        in_specs=[pl.BlockSpec(memory_space=pltpu.SMEM)]
        + [pl.BlockSpec(memory_space=pl.ANY)] * inputs,
        out_specs=[pl.BlockSpec(memory_space=pltpu.VMEM)] * 2,
        scratch_shapes=[
            pltpu.VMEM((layers, chips, tokens, width), kind),
            pltpu.VMEM((SIDE, holders, all_rows, tokens), kind),
            pltpu.SemaphoreType.DMA((layers, inputs)),
        ],
        out_shape=[shape, shape],
        compiler_params=pltpu.CompilerParams(vmem_limit_bytes=50 * MIB),
        cost_estimate=pl.CostEstimate(flops=0, bytes_accessed=1024, transcendentals=0),
        name="gradient_partials",
    )(here, *pieces, *parts)


def deal_kernel(slot_ref, kept_ref, got_ref, out_ref):
    layer, half = pl.program_id(0), pl.program_id(1)
    holders, rows, _ = kept_ref.shape
    piece = out_ref.shape[1]
    cols = rows // piece
    for holder in range(holders):
        total = kept_ref[holder].astype(jnp.float32) + got_ref[holder].astype(jnp.float32)
        total = total.astype(out_ref.dtype)
        for col in range(cols):
            slot = slot_ref[((half * holders + holder) * 2 + layer) * cols + col]
            out_ref[slot] = total[col * piece : (col + 1) * piece]


def deal_to_slots(slots, kept, got, slot_total):
    holders, all_rows, size = kept.shape
    layers = 2
    rows = all_rows // layers
    shape = (holders * slot_total, TABLE_ROWS, size)
    return pl.pallas_call(
        deal_kernel,
        grid_spec=pltpu.PrefetchScalarGridSpec(
            num_scalar_prefetch=1,
            grid=(layers, 2),
            in_specs=[pl.BlockSpec((holders // 2, rows, size), lambda l, h, s: (h, l, 0))] * 2,
            out_specs=pl.BlockSpec(shape, lambda l, h, s: (0, 0, 0)),
        ),
        out_shape=jax.ShapeDtypeStruct(shape, kept.dtype),
        compiler_params=pltpu.CompilerParams(vmem_limit_bytes=6 * MIB),
        cost_estimate=pl.CostEstimate(flops=0, bytes_accessed=1024, transcendentals=0),
        name="deal_to_slots",
    )(slots, kept, got)


def slot_kernel(source_ref, left_ref, right_ref, first_ref, second_ref, *refs):
    out_ref, left_stat_ref, right_stat_ref, lefts, rights, turns, sems = refs
    slot = pl.program_id(0)
    slot_total, size, _ = lefts.shape

    def fetches(s):
        moves = [(left_ref.at[s], lefts.at[s]), (right_ref.at[s], rights.at[s])]
        moves += [(ref.at[:, s], turns.at[s, q]) for q, ref in enumerate((first_ref, second_ref))]
        return [pltpu.make_async_copy(*move, sems.at[s, n]) for n, move in enumerate(moves)]

    @pl.when(slot == 0)
    def _():
        for s in range(slot_total):
            for fetch in fetches(s):
                fetch.start()

    for fetch in fetches(slot):
        fetch.wait()
    is_live = source_ref[slot] >= 0

    @pl.when(is_live)
    def _():
        turned = turns[slot].reshape(size, size)
        inner = dot(lefts[slot], turned, NT).astype(out_ref.dtype)
        out_ref[0] = dot(inner, rights[slot], NN).astype(out_ref.dtype)
        scale = 1.0 / size
        left_stat_ref[0] = (dot(turned, turned, TN) * scale).astype(left_stat_ref.dtype)
        right_stat_ref[0] = (dot(turned, turned, NT) * scale).astype(right_stat_ref.dtype)

    @pl.when(jnp.logical_not(is_live))
    def _():
        left_stat_ref[...] = jnp.zeros_like(left_stat_ref)
        right_stat_ref[...] = jnp.zeros_like(right_stat_ref)


def work_on_slots(sources, left_roots, right_roots, arrived, owner_total):
    slot_total, size, _ = left_roots.shape
    kind = left_roots.dtype
    slices = arrived[0].shape

    def out_place(s, source):
        place = source[s]
        for back in range(1, slot_total):
            place = jnp.where(place >= 0, place, source[jnp.maximum(s - back, 0)])
        return (place, 0, 0)

    def live(s, source):
        return (s, 0, 0)

    stats = jax.ShapeDtypeStruct((slot_total, size, size), kind)
    return pl.pallas_call(
        slot_kernel,
        grid_spec=pltpu.PrefetchScalarGridSpec(
            num_scalar_prefetch=1,
            grid=(slot_total,),
            in_specs=[pl.BlockSpec(memory_space=pl.ANY)] * 4,
            out_specs=[
                pl.BlockSpec((1, size, size), out_place),
                pl.BlockSpec((1, size, size), live),
                pl.BlockSpec((1, size, size), live),
            ],
            scratch_shapes=[
                pltpu.VMEM((slot_total, size, size), kind),
                pltpu.VMEM((slot_total, size, size), kind),
                pltpu.VMEM((slot_total, CHUNKS, slices[0], slices[2], size), kind),
                pltpu.SemaphoreType.DMA((slot_total, 4)),
            ],
        ),
        out_shape=[jax.ShapeDtypeStruct((owner_total, size, size), kind), stats, stats],
        compiler_params=pltpu.CompilerParams(vmem_limit_bytes=36 * MIB),
        cost_estimate=pl.CostEstimate(
            flops=8 * slot_total * size**3,
            bytes_accessed=12 * slot_total * size * size,
            transcendentals=0,
        ),
        name="work_on_slots",
    )(sources, left_roots, right_roots, *arrived)


def place_kernel(owner_ref, returned_ref, out_ref, held, in_sems, out_sems):
    layers, size, width = out_ref.shape
    cols = width // size
    blocks = [(l, c, l * cols + c) for l in range(layers) for c in range(cols)]
    fetches = [
        pltpu.make_async_copy(returned_ref.at[owner_ref[t]], held.at[t], in_sems.at[t])
        for _, _, t in blocks
    ]
    stores = [
        pltpu.make_async_copy(
            held.at[t], out_ref.at[l, :, pl.ds(c * size, size)], out_sems.at[t]
        )
        for l, c, t in blocks
    ]
    for fetch in fetches:
        fetch.start()
    for fetch, store in zip(fetches, stores):
        fetch.wait()
        store.start()
    for store in stores:
        store.wait()


def place_blocks(owners, returned, layers, cols):
    _, size, _ = returned.shape
    return pl.pallas_call(
        place_kernel,
        in_specs=[
            pl.BlockSpec(memory_space=pltpu.SMEM),
            pl.BlockSpec(memory_space=pl.ANY),
        ],
        out_specs=pl.BlockSpec(memory_space=pl.ANY),
        out_shape=jax.ShapeDtypeStruct((layers, size, cols * size), returned.dtype),
        scratch_shapes=[
            pltpu.VMEM((layers * cols, size, size), returned.dtype),
            pltpu.SemaphoreType.DMA((layers * cols,)),
            pltpu.SemaphoreType.DMA((layers * cols,)),
        ],
        compiler_params=pltpu.CompilerParams(vmem_limit_bytes=8 * MIB),
        cost_estimate=pl.CostEstimate(
            flops=0, bytes_accessed=4 * layers * cols * size * size, transcendentals=0
        ),
        name="place_blocks",
    )(owners, returned)


def activations_for_chips(activations, chip_y, parity):
    layers, tokens, width = activations.shape
    rows, pair_width = tokens // 4, width // SIDE
    return [
        jnp.stack(
            [
                lax.dynamic_slice(
                    activations,
                    (0, (parity * 2 + u) * rows, lax.rem(chip_y + hops, SIDE) * pair_width),
                    (layers, rows, pair_width),
                )
                for u in range(2)
            ]
        )
        for hops in (0, 1, SIDE - 1, 2)
    ]


def on_device(
    activations, cotangents, left_root, right_root, block_owner, owned_sources, owner_counts
):
    owner_total = lax.axis_size("mp")
    layers, _, width = cotangents.shape
    slot_total, size = left_root.shape[2], left_root.shape[-1]
    cols = width // size
    blocks = layers * cols
    owners = block_owner.reshape(-1)
    group, holder = lax.axis_index("dp"), lax.axis_index("mp")
    chip_y, core = group // CORES, lax.rem(group, CORES)
    parity = lax.rem(holder, 2)

    for_chips = activations_for_chips(activations, chip_y, parity)
    from_chips = [for_chips[0]] + [
        along_y(piece, hops) for piece, hops in zip(for_chips[1:], (1, -1, 2))
    ]
    first, second = split_cotangents(owners, after(cotangents, *for_chips), owner_total)
    first = exchange(first)
    second = exchange(after(second, first))
    base = first.shape[1]

    halves = [jnp.stack([piece[u] for piece in from_chips]) for u in range(2)]
    first_parts = ring_in_two(first, along_y)
    pieces = (halves[0], halves[1], along_z(halves[0], 1), along_z(halves[1], -1))
    owner_of = second[:, base : base + blocks, 0].astype(jnp.int32)

    all_owners = jnp.arange(owner_total, dtype=jnp.int32)
    named = (owner_of[:, :, None] == all_owners).astype(jnp.int32)
    given = jnp.sum(named, axis=1)
    earlier = (all_owners[:, None] > all_owners[None, :]).astype(jnp.int32)
    slot_of = jnp.sum(earlier[:, :, None] * given[None, :, :], axis=1)
    slots = (owner_of * slot_total + jnp.sum(named * slot_of[:, None, :], axis=-1)).reshape(-1)

    def sliced_slots(here, parts):
        kept, given = gradient_partials(here, pieces, parts)
        return deal_to_slots(slots, kept, other_core(given), slot_total)

    slot_range = jnp.arange(slot_total, dtype=jnp.int32)
    sources = jnp.where(slot_range < owner_counts.reshape(()), owned_sources.reshape(-1), -1)
    here = jnp.stack((core, parity)).astype(jnp.int32)
    here, slots, sources, second = lax.optimization_barrier(
        (here, slots, sources, second[:, :base], first_parts[1:3])
    )[:4]
    second_parts = (second, along_y(second, 1), along_y(second, -1), along_y(second, 2))
    dealt = sliced_slots(here, first_parts)
    arrived = exchange(dealt)
    dealt = sliced_slots(after(here, dealt), second_parts)
    dealt, arrived = lax.optimization_barrier((dealt, arrived))
    more = exchange(dealt)

    def by_slot(value):
        return value.reshape((owner_total, slot_total) + value.shape[1:])

    returning, left_stats, right_stats = work_on_slots(
        sources,
        left_root.reshape(slot_total, size, size),
        right_root.reshape(slot_total, size, size),
        (by_slot(arrived), by_slot(more)),
        owner_total,
    )
    precond = place_blocks(owners, exchange(returning), layers, cols)
    stat_shape = (1, 1, slot_total, size, size)
    return (precond, left_stats.reshape(stat_shape), right_stats.reshape(stat_shape))


def solution(mesh):
    placed = (
        P(None, "dp", None),
        P(None, "dp", "mp"),
        P("dp", "mp", None, None, None),
        P("dp", "mp", None, None, None),
        P("dp", "mp", None),
        P("dp", "mp", None),
        P("dp", "mp"),
    )
    return jax.shard_map(
        on_device,
        mesh=mesh,
        in_specs=placed,
        out_specs=(
            P(None, "dp", "mp"),
            P("dp", "mp", None, None, None),
            P("dp", "mp", None, None, None),
        ),
        check_vma=False,
    )
```
